32 devices in a mesh: pipe: 2 (over x), expert: 16 (over z, y, core).
Axes of the slice: x: 2, y: 2, z: 4, core: 2. Of those that a mesh axis runs over, the one named last changes fastest.
Arguments:
- inputs: bfloat16 [2, 2048, 2048], P('pipe', 'expert'), may hold values from -6 to 6
- out_grads: bfloat16 [2, 2048, 2048], P('pipe', 'expert'), may hold values from -6 to 6
- expert_ids: int32 [2, 2048, 8], P('pipe', 'expert'), may hold values from 0 to 127, all different within a row
- gate_values: float32 [2, 2048, 8], P('pipe', 'expert'), may hold values from 0.2 to 1
- w_gate: bfloat16 [2, 2048, 4096], P('pipe', None, 'expert'), may hold values from -0.125 to 0.125
- w_up: bfloat16 [2, 2048, 4096], P('pipe', None, 'expert'), may hold values from -0.125 to 0.125
- w_down: bfloat16 [2, 4096, 2048], P('pipe', 'expert'), may hold values from -0.1875 to 0.1875
Outputs:
- prev_grads: bfloat16 [2, 2048, 2048], P('pipe', 'expert')
- gate_grads: float32 [2, 2048, 8], P('pipe', 'expert')
The draws below stay inside these ranges and needn't reach their ends.
Inputs may be any that keep to these rules, and one draw needn't show every extreme that they name: `expert_ids`: each token names 8 different experts.
All inputs are finite; a program needn't handle non-finite values.
Results may differ from the reference program's by a relative error of at most 0.0057.
Values may be sent and summed in bfloat16 or wider, within the bound.
No kernel may reach another device: no remote copies, remote signals or barrier semaphores. Data moves between devices by JAX's collectives and lax.ppermute only.
A program may use at most 64 MiB of HBM per device.

```python
import jax
import jax.numpy as jnp
from jax import lax

D = 2048
FF = 1024
EXPERTS_ALL = 128
TOPK = 8
SLICES = 4
TOK_DEV = 128
CAP = 12
EXP_FLIGHT = 4
SECTIONS = 2
TOKENS = 2048
N_EXPERT = 16


def steps_of(rng, dims, cuts, low, high):
    def one(dim, shards_of):
        steps = jax.random.uniform(jax.random.fold_in(jax.random.fold_in(rng, 6), dim), (shards_of,), jnp.float32, low / len(cuts), high / len(cuts))
        return jnp.repeat(jnp.exp(steps), dims[dim] // shards_of).reshape((-1,) + (1,) * (len(dims) - dim - 1))

    level = one(*cuts[0])
    for cut in cuts[1:]:
        level = level * one(*cut)
    return level


def different_ones(own_key, rows, amount, top, lift):
    ranking = jax.random.permutation(jax.random.fold_in(own_key, 1), amount)
    favour = ranking
    for power in range(3):
        favour = favour * favour // amount
    favour = favour * lift // amount
    tickets = jax.random.randint(jax.random.fold_in(own_key, 2), (rows, amount), 0, 4096) + favour
    holders = jax.random.permutation(jax.random.fold_in(own_key, 3), rows)[jnp.arange(amount) % rows]
    tickets = jnp.where(jnp.arange(rows)[:, None] == holders[None, :], 1 << 14, tickets)
    priority = tickets * amount + jnp.arange(amount)
    return lax.top_k(priority.astype(jnp.int32), top)[1].astype(jnp.int32)


def centred(stream_key, extent, spread, most, cuts=(), kind=jnp.bfloat16):
    entries = spread * jax.random.normal(stream_key, extent, jnp.float32)
    if cuts:
        entries = entries * steps_of(stream_key, extent, cuts, -0.22, 0.18)
    return jnp.clip(entries, -most, most).astype(kind)


def setup_inputs(seed: int = 0) -> dict:
    splits = jax.random.split(jax.random.key(seed), 8)
    return {
        "inputs": centred(splits[0], (SECTIONS, TOKENS, D), 1.0, 6.0, ((0, 2), (1, 16))),
        "out_grads": centred(splits[1], (SECTIONS, TOKENS, D), 1.0, 6.0, ((0, 2), (1, 16))),
        "expert_ids": different_ones(splits[2], SECTIONS * TOKENS, EXPERTS_ALL, TOPK, 1024).reshape((SECTIONS, TOKENS, TOPK)),
        "gate_values": jnp.clip(0.2 + 0.8 * jax.random.uniform(splits[3], (SECTIONS, TOKENS, TOPK), jnp.float32) ** steps_of(splits[3], (SECTIONS, TOKENS, TOPK), ((0, 2), (1, 16)), -0.2, 0.2), 0.2, 1.0),
        "w_gate": centred(splits[4], (SECTIONS, D, EXP_FLIGHT * FF), D ** -0.5, 0.125, ((0, 2), (2, 16))),
        "w_up": centred(splits[5], (SECTIONS, D, EXP_FLIGHT * FF), D ** -0.5, 0.125, ((0, 2), (2, 16))),
        "w_down": centred(splits[6], (SECTIONS, EXP_FLIGHT * FF, D), FF ** -0.5, 0.1875, ((0, 2), (1, 16))),
    }


def expert_grads(rows_in, rows_grad, gate_cols, up_cols, down_rows):
    gate_pre = jnp.dot(rows_in, gate_cols, preferred_element_type=jnp.float32)
    up_pre = jnp.dot(rows_in, up_cols, preferred_element_type=jnp.float32)
    sig = jax.nn.sigmoid(gate_pre)
    act = gate_pre * sig
    hidden = act * up_pre
    dhidden = jnp.dot(rows_grad, down_rows.T, preferred_element_type=jnp.float32)
    gate_part = jnp.sum(hidden * dhidden, axis=1)
    d_gate_pre = (dhidden * up_pre * sig * (1.0 + gate_pre * (1.0 - sig))).astype(jnp.bfloat16)
    d_up_pre = (dhidden * act).astype(jnp.bfloat16)
    back = jnp.dot(d_gate_pre, gate_cols.T, preferred_element_type=jnp.float32)
    back = back + jnp.dot(d_up_pre, up_cols.T, preferred_element_type=jnp.float32)
    return back, gate_part


def section_grads(tokens, grads, ids, gates, w_gate, w_up, w_down):
    blocks = N_EXPERT
    flight = N_EXPERT // SLICES
    tok = tokens.reshape(blocks, TOK_DEV, D)
    grd = grads.reshape(blocks, TOK_DEV, D)
    idb = ids.reshape(blocks, TOK_DEV, TOPK)
    gtb = gates.reshape(blocks, TOK_DEV, TOPK)
    experts_here = jnp.arange(flight, dtype=jnp.int32)
    match = idb[:, :, :, None] == experts_here[None, None, None, :]
    routed = jnp.sum(match.astype(jnp.int32), axis=2)
    weight_te = jnp.sum(jnp.where(match, gtb[:, :, :, None], jnp.float32(0.0)), axis=2)
    before = jnp.cumsum(routed, axis=1) - routed
    kept = (routed > 0) & (before < CAP)
    slots = jnp.arange(CAP, dtype=jnp.int32)
    keptt = jnp.transpose(kept, (0, 2, 1))
    beforet = jnp.transpose(before, (0, 2, 1))
    place = (keptt[:, :, None, :] & (beforet[:, :, None, :] == slots[None, None, :, None])).astype(jnp.float32)
    rows_x = jnp.einsum('bect,btd->ebcd', place, tok.astype(jnp.float32)).astype(jnp.bfloat16)
    rows_g = jnp.einsum('bect,btd->ebcd', place, grd.astype(jnp.float32)).astype(jnp.bfloat16)
    width_dev = FF // SLICES

    def one_expert(e):
        flat_x = rows_x[e].reshape(blocks * CAP, D)
        flat_g = rows_g[e].reshape(blocks * CAP, D)
        back_sum = jnp.zeros((blocks * CAP, D), jnp.float32)
        part_sum = jnp.zeros((blocks * CAP,), jnp.float32)
        for piece in range(SLICES):
            start = (e * FF + piece * width_dev).astype(jnp.int32)
            gate_cols = lax.dynamic_slice_in_dim(w_gate, start, width_dev, 1)
            up_cols = lax.dynamic_slice_in_dim(w_up, start, width_dev, 1)
            down_rows = lax.dynamic_slice_in_dim(w_down, start, width_dev, 0)
            back, part = expert_grads(flat_x, flat_g, gate_cols, up_cols, down_rows)
            back_bf = lax.optimization_barrier(back.astype(jnp.bfloat16))
            part_bf = lax.optimization_barrier(part.astype(jnp.bfloat16))
            back_sum = back_sum + back_bf.astype(jnp.float32)
            part_sum = part_sum + part_bf.astype(jnp.float32)
        return back_sum.reshape(blocks, CAP, D), part_sum.reshape(blocks, CAP)

    total, gsum = lax.map(one_expert, experts_here)
    mix = place * jnp.transpose(weight_te, (0, 2, 1))[:, :, None, :]
    moe = jnp.einsum('bect,ebcd->btd', mix, total, precision=lax.Precision.HIGHEST)
    d_gate_te = jnp.einsum('bect,ebc->bte', place, gsum, precision=lax.Precision.HIGHEST)
    d_gates = jnp.sum(jnp.where(match, d_gate_te[:, :, None, :], jnp.float32(0.0)), axis=3)
    return moe.astype(jnp.bfloat16).reshape(TOKENS, D), d_gates.reshape(TOKENS, TOPK)


def reference(inputs, out_grads, expert_ids, gate_values, w_gate, w_up, w_down):
    moes = []
    gradg = []
    for section in range(SECTIONS):
        moe, dg = section_grads(inputs[section], out_grads[section], expert_ids[section], gate_values[section], w_gate[section], w_up[section], w_down[section])
        moes.append(moe)
        gradg.append(dg)
    moe_all = jnp.stack(moes, axis=0)
    prev_grads = jnp.concatenate([moe_all[1:], moe_all[:1]], axis=0)
    return prev_grads, jnp.stack(gradg, axis=0)
```

```python
import functools

import jax
import jax.numpy as jnp
from jax import lax
from jax.experimental import pallas as pl
from jax.experimental.pallas import tpu as pltpu
from jax.sharding import PartitionSpec as P

SLICES = 4
CAP = 12
PAD = 16
LANES = 128
BF = jnp.bfloat16
F32 = jnp.float32
PARAMS = pltpu.CompilerParams(vmem_limit_bytes=40 * 1024 * 1024)


def select_kernel(flight, ids_ref, gates_ref, x_ref, g_ref, *outs):
    blocks, mix_ref, place_ref = outs[:flight], outs[flight], outs[flight + 1]
    own = lax.axis_index("expert") // SLICES
    ids = ids_ref[...]
    gates = gates_ref[...]
    count = ids.shape[1]
    routed, weight = [], []
    for s in range(flight):
        match = ids == (own ^ s)
        routed.append(jnp.sum(jnp.where(match, 1.0, 0.0), axis=0, keepdims=True))
        weight.append(jnp.sum(jnp.where(match, gates, 0.0), axis=0, keepdims=True))
    fill = [jnp.zeros((1, count), F32)] * (-flight % 8)
    table = jnp.concatenate(routed + fill, axis=0)
    earlier = lax.broadcasted_iota(jnp.int32, (count, count), 0) < lax.broadcasted_iota(
        jnp.int32, (count, count), 1
    )
    rank = jnp.dot(
        table.astype(BF), jnp.where(earlier, 1.0, 0.0).astype(BF), preferred_element_type=F32
    )
    key = jnp.where((table > 0.0) & (rank < float(CAP)), rank, -1.0)
    row = lax.broadcasted_iota(jnp.int32, (2 * CAP, count), 0)
    is_x = row < CAP
    slot = jnp.where(is_x, row, row - CAP).astype(F32)
    slot16 = lax.broadcasted_iota(jnp.int32, (PAD, count), 0)
    slot16 = jnp.where(slot16 < CAP, slot16, -2).astype(F32)
    picks_x, picks_g = [], []
    for s in range(flight):
        hit = key[s : s + 1] == slot
        picks_x.append(jnp.where(hit & is_x, 1.0, 0.0))
        picks_g.append(jnp.where(hit & ~is_x, 1.0, 0.0))
        at = jnp.where(key[s : s + 1] == slot16, 1.0, 0.0)
        place_ref[s * PAD : (s + 1) * PAD] = at
        mix_ref[s * PAD : (s + 1) * PAD] = at * weight[s]
    pick_x = jnp.concatenate(picks_x, axis=0).astype(BF)
    pick_g = jnp.concatenate(picks_g, axis=0).astype(BF)
    rows = jnp.dot(pick_x, x_ref[...], preferred_element_type=F32)
    rows = rows + jnp.dot(pick_g, g_ref[...], preferred_element_type=F32)
    rows = rows.astype(BF)
    for s in range(flight):
        blocks[s][...] = rows[s * 2 * CAP : (s + 1) * 2 * CAP]


def experts_kernel(count, *refs):
    blocks, weights, outs = refs[:count], refs[count : count + 6], refs[count + 6 :]
    x = jnp.concatenate([b[:CAP] for b in blocks], axis=0)
    g = jnp.concatenate([b[CAP:] for b in blocks], axis=0)
    width = x.shape[1]
    nt = (((1,), (1,)), ((), ()))
    part = jnp.zeros((x.shape[0], 1), F32)
    lefts, rights = [], []
    for half in range(2):
        wg, wu, wd = weights[3 * half : 3 * half + 3]
        a = jnp.dot(x, wg[...], preferred_element_type=F32)
        u = jnp.dot(x, wu[...], preferred_element_type=F32)
        dh = lax.dot_general(g, wd[...], nt, preferred_element_type=F32)
        sig = jax.nn.sigmoid(a)
        act = a * sig
        part = part + jnp.sum(act * u * dh, axis=1, keepdims=True)
        lefts += [
            (dh * u * sig * (1.0 + a * (1.0 - sig))).astype(BF),
            (dh * act).astype(BF),
        ]
        rights += [wg, wu]
    part_hi = part.astype(BF).astype(F32)
    lane = lax.broadcasted_iota(jnp.int32, (x.shape[0], LANES), 1)
    tail = jnp.where(lane == 0, part_hi, jnp.where(lane == 1, part - part_hi, 0.0))
    main = width * CAP // PAD
    step = width - main
    pieces = []
    for c in range(0, width, step):
        total = lax.dot_general(lefts[0], rights[0][c : c + step, :], nt, preferred_element_type=F32)
        for left, right in zip(lefts[1:], rights[1:]):
            total = total + lax.dot_general(left, right[c : c + step, :], nt, preferred_element_type=F32)
        pieces.append(total)
    last = pieces[-1]
    extra = PAD - CAP
    for i in range(count):
        base = i * CAP
        for j, piece in enumerate(pieces[:-1]):
            under = last[base + extra * j : base + extra * (j + 1)]
            both = jnp.concatenate([piece[base : base + CAP], under], axis=0)
            outs[i][:, j * step : (j + 1) * step] = both.astype(BF)
        both = jnp.concatenate([tail[base : base + CAP], jnp.zeros((extra, LANES), F32)], axis=0)
        outs[i][:, main:] = both.astype(BF)


def tails_kernel(flight, *refs):
    blocks, out_ref = refs[:-1], refs[-1]
    for s in range(flight):
        tail = blocks[s][...].astype(F32) + blocks[s + flight][...].astype(F32)
        out_ref[s * PAD : (s + 1) * PAD] = tail


def split(value):
    high = value.astype(BF)
    return high, (value - high.astype(F32)).astype(BF)


def mix_kernel(flight, *refs):
    blocks, mix_ref, out_ref = refs[: 2 * flight], refs[2 * flight], refs[2 * flight + 1]
    width = out_ref.shape[1]
    main = width * CAP // PAD
    step = width - main
    extra = PAD - CAP
    tn = (((0,), (0,)), ((), ()))
    mix_hi, mix_lo = split(mix_ref[...])
    left = jnp.concatenate([mix_hi, mix_hi, mix_lo], axis=0)

    def blend(rows):
        high, low = split(rows)
        right = jnp.concatenate([high, low, high], axis=0)
        return lax.dot_general(left, right, tn, preferred_element_type=F32).astype(BF)

    lasts = []
    for j in range(main // step):
        cols = pl.ds(j * step, step)
        rows = jnp.concatenate(
            [
                blocks[s][:, cols].astype(F32) + blocks[s + flight][:, cols].astype(F32)
                for s in range(flight)
            ],
            axis=0,
        )
        out_ref[:, j * step : (j + 1) * step] = blend(rows)
        lasts.append([rows[s * PAD + CAP : (s + 1) * PAD] for s in range(flight)])
    zero = jnp.zeros((extra, step), F32)
    rows = jnp.concatenate(
        [piece for s in range(flight) for piece in [l[s] for l in lasts] + [zero]], axis=0
    )
    out_ref[:, main:] = blend(rows)


def gates_kernel(flight, ids_ref, place_ref, tail_ref, out_ref):
    own = lax.axis_index("expert") // SLICES
    ids = ids_ref[...]
    total = jnp.zeros(ids.shape, F32)
    for s in range(flight):
        q = jnp.sum(tail_ref[s * PAD : (s + 1) * PAD], axis=1, keepdims=True)
        back = jnp.sum(place_ref[s * PAD : (s + 1) * PAD] * q, axis=0, keepdims=True)
        total = total + jnp.where(ids == (own ^ s), back, 0.0)
    out_ref[...] = total


def moved(value, sections, devices, stage, flip, bits):
    route = []
    for p in range(sections):
        for e in range(devices):
            route.append((p * devices + e, (p + flip) % sections * devices + (e ^ bits)))
    return lax.ppermute(value, stage, route)


def per_device(inputs, out_grads, expert_ids, gate_values, w_gate, w_up, w_down):
    devices = lax.axis_size("expert")
    sections = lax.axis_size("pipe")
    flight = devices // SLICES
    count, width = inputs.shape[1:]
    axes = ("pipe", "expert")
    go = functools.partial(moved, sections=sections, devices=devices, stage=axes)
    own_weights = [w_gate[0], w_up[0], w_down[0]]
    near_weights = [go(w, flip=0, bits=1) for w in own_weights]
    ids = expert_ids[0].T
    gates = gate_values[0].T
    *blocks, mix, place = pl.pallas_call(
        functools.partial(select_kernel, flight),
        out_shape=[jax.ShapeDtypeStruct((2 * CAP, width), BF)] * flight
        + [jax.ShapeDtypeStruct((flight * PAD, count), F32)] * 2,
        compiler_params=PARAMS,
        name="select",
    )(ids, gates, inputs[0], out_grads[0])
    rows = [blocks[0]] + [go(blocks[s], flip=0, bits=SLICES * s) for s in range(1, flight)]
    rows = rows + [go(r, flip=0, bits=2) for r in rows]
    mix = go(mix, flip=-1, bits=0)
    main = width * CAP // PAD
    parts = pl.pallas_call(
        functools.partial(experts_kernel, 2 * flight),
        out_shape=[jax.ShapeDtypeStruct((PAD, main + LANES), BF)] * (2 * flight),
        compiler_params=PARAMS,
        name="experts",
    )(*rows, *own_weights, *near_weights)
    home = [
        go(parts[t * flight + s], flip=-1, bits=SLICES * s + 2 * t)
        for t in range(2)
        for s in range(flight)
    ]
    tails = pl.pallas_call(
        functools.partial(tails_kernel, flight),
        out_shape=jax.ShapeDtypeStruct((flight * PAD, LANES), F32),
        compiler_params=PARAMS,
        name="tails",
    )(*[h[:, main:] for h in home])
    tails = go(tails, flip=1, bits=0)
    moe = pl.pallas_call(
        functools.partial(mix_kernel, flight),
        out_shape=jax.ShapeDtypeStruct((count, width), BF),
        compiler_params=PARAMS,
        name="mix",
    )(*home, mix)
    d_gates = pl.pallas_call(
        functools.partial(gates_kernel, flight),
        out_shape=jax.ShapeDtypeStruct(ids.shape, F32),
        compiler_params=PARAMS,
        name="gates",
    )(ids, place, tails)
    return (moe[None], d_gates.T[None])


def solution(mesh):
    return jax.shard_map(
        per_device,
        mesh=mesh,
        in_specs=(
            P("pipe", "expert", None),
            P("pipe", "expert", None),
            P("pipe", "expert", None),
            P("pipe", "expert", None),
            P("pipe", None, "expert"),
            P("pipe", None, "expert"),
            P("pipe", "expert", None),
        ),
        out_specs=(P("pipe", "expert", None), P("pipe", "expert", None)),
        check_vma=False,
    )
```

```python
import functools

import jax
import jax.numpy as jnp
from jax import lax
from jax.experimental import pallas as pl
from jax.experimental.pallas import tpu as pltpu
from jax.sharding import PartitionSpec as P

SLICES = 4
CAP = 12
PAD = 16
LANES = 128
BF = jnp.bfloat16
F32 = jnp.float32
PARAMS = pltpu.CompilerParams(vmem_limit_bytes=40 * 1024 * 1024)


def split(value):
    high = value.astype(BF)
    return high, (value - high.astype(F32)).astype(BF)


def select_kernel(flight, ids_hbm, gates_hbm, x_hbm, g_hbm, wg_hbm, wu_hbm, wd_hbm, *refs):
    blocks, (mix_ref, place_ref, pack_ref) = refs[:flight], refs[flight : flight + 3]
    ids_ref, gates_ref, x_ref, g_ref, sems = refs[flight + 3 :]
    width, hidden = wg_hbm.shape
    first = [
        pltpu.make_async_copy(src, dst, sems.at[i])
        for i, (src, dst) in enumerate(
            [(ids_hbm, ids_ref), (gates_hbm, gates_ref), (x_hbm, x_ref), (g_hbm, g_ref)]
        )
    ]
    later = [
        pltpu.make_async_copy(wg_hbm, pack_ref.at[pl.ds(0, width)], sems.at[4]),
        pltpu.make_async_copy(wu_hbm, pack_ref.at[pl.ds(width, width)], sems.at[5]),
    ]
    for k in range(width // hidden):
        part = pack_ref.at[pl.ds(2 * width + k * hidden, hidden)]
        later.append(pltpu.make_async_copy(wd_hbm.at[:, pl.ds(k * hidden, hidden)], part, sems.at[6 + k]))
    for copy in first + later:
        copy.start()
    own = lax.axis_index("expert") // SLICES
    first[0].wait()
    first[1].wait()
    ids = ids_ref[...]
    gates = gates_ref[...]
    count = ids.shape[1]
    routed, weight = [], []
    for s in range(flight):
        match = ids == (own ^ s)
        routed.append(jnp.sum(jnp.where(match, 1.0, 0.0), axis=0, keepdims=True))
        weight.append(jnp.sum(jnp.where(match, gates, 0.0), axis=0, keepdims=True))
    fill = [jnp.zeros((1, count), F32)] * (-flight % 8)
    table = jnp.concatenate(routed + fill, axis=0)
    earlier = lax.broadcasted_iota(jnp.int32, (count, count), 0) < lax.broadcasted_iota(
        jnp.int32, (count, count), 1
    )
    rank = jnp.dot(
        table.astype(BF), jnp.where(earlier, 1.0, 0.0).astype(BF), preferred_element_type=F32
    )
    key = jnp.where((table > 0.0) & (rank < float(CAP)), rank, -1.0)
    row = lax.broadcasted_iota(jnp.int32, (2 * CAP, count), 0)
    is_x = row < CAP
    slot = jnp.where(is_x, row, row - CAP).astype(F32)
    slot16 = lax.broadcasted_iota(jnp.int32, (PAD, count), 0)
    slot16 = jnp.where(slot16 < CAP, slot16, -2).astype(F32)
    picks_x, picks_g = [], []
    for s in range(flight):
        hit = key[s : s + 1] == slot
        picks_x.append(jnp.where(hit & is_x, 1.0, 0.0))
        picks_g.append(jnp.where(hit & ~is_x, 1.0, 0.0))
        at = jnp.where(key[s : s + 1] == slot16, 1.0, 0.0)
        place_ref[s * PAD : (s + 1) * PAD] = at
        for i, value in enumerate(split(at * weight[s])):
            mix_ref[:, (2 * s + i) * count : (2 * s + i + 1) * count] = value
    pick_x = jnp.concatenate(picks_x, axis=0).astype(BF)
    pick_g = jnp.concatenate(picks_g, axis=0).astype(BF)
    first[2].wait()
    rows = jnp.dot(pick_x, x_ref[...], preferred_element_type=F32)
    first[3].wait()
    rows = rows + jnp.dot(pick_g, g_ref[...], preferred_element_type=F32)
    rows = rows.astype(BF)
    for s in range(flight):
        blocks[s][...] = rows[s * 2 * CAP : (s + 1) * 2 * CAP]
    for copy in later:
        copy.wait()


def hidden_kernel(flight, *refs):
    blocks, packs = refs[: 2 * flight], refs[2 * flight : 2 * flight + 2]
    left_ref, part_ref = refs[2 * flight + 2 :]
    x = jnp.concatenate([b[:CAP] for b in blocks], axis=0)
    g = jnp.concatenate([b[CAP:] for b in blocks], axis=0)
    width = x.shape[1]
    hidden = packs[0].shape[1]
    nt = (((1,), (1,)), ((), ()))
    part = jnp.zeros((x.shape[0], 1), F32)
    for half, pack in enumerate(packs):
        a = jnp.dot(x, pack[:width], preferred_element_type=F32)
        u = jnp.dot(x, pack[width : 2 * width], preferred_element_type=F32)
        dh = jnp.zeros_like(a)
        for k in range(0, width, hidden):
            down = pack[2 * width + k : 2 * width + k + hidden]
            dh = dh + lax.dot_general(g[:, k : k + hidden], down, nt, preferred_element_type=F32)
        sig = jax.nn.sigmoid(a)
        act = a * sig
        part = part + jnp.sum(act * u * dh, axis=1, keepdims=True)
        at = 2 * half * hidden
        left_ref[:, at : at + hidden] = (dh * u * sig * (1.0 + a * (1.0 - sig))).astype(BF)
        left_ref[:, at + hidden : at + 2 * hidden] = (dh * act).astype(BF)
    high, low = split(part)
    high, low = high.astype(F32), low.astype(F32)
    lane = lax.broadcasted_iota(jnp.int32, (CAP, LANES), 1)
    tail = jnp.zeros((CAP, LANES), F32)
    for i in range(2 * flight):
        rows = slice(i * CAP, (i + 1) * CAP)
        tail = jnp.where(lane == 2 * i, high[rows], jnp.where(lane == 2 * i + 1, low[rows], tail))
    part_ref[...] = jnp.concatenate([tail, jnp.zeros((PAD - CAP, LANES), F32)], axis=0).astype(BF)


def inputs_kernel(flight, left_ref, own_ref, near_ref, keep_ref, send_ref):
    hidden = own_ref.shape[1]
    width = own_ref.shape[0] // 3
    nt = (((1,), (1,)), ((), ()))
    main = width * CAP // PAD
    step = width - main
    extra = PAD - CAP
    pieces = []
    for c in range(0, width, step):
        total = jnp.zeros((left_ref.shape[0], step), F32)
        for i in range(4):
            pack = (own_ref, near_ref)[i // 2]
            right = pack[i % 2 * width + c : i % 2 * width + c + step]
            left = left_ref[:, i * hidden : (i + 1) * hidden]
            total = total + lax.dot_general(left, right, nt, preferred_element_type=F32)
        pieces.append(total)
    last = pieces[-1]
    for i in range(2 * flight):
        base = i * CAP
        out_ref = (keep_ref, send_ref)[i // flight]
        at = i % flight * PAD
        for j, piece in enumerate(pieces[:-1]):
            under = last[base + extra * j : base + extra * (j + 1)]
            both = jnp.concatenate([piece[base : base + CAP], under], axis=0)
            out_ref[at : at + PAD, j * step : (j + 1) * step] = both.astype(out_ref.dtype)


def attach_kernel(flight, part_ref, keep_ref, send_ref, keep_out, send_out):
    del keep_ref, send_ref
    part = part_ref[...].astype(F32)
    lane = lax.broadcasted_iota(jnp.int32, part.shape, 1)
    for i in range(2 * flight):
        out_ref = (keep_out, send_out)[i // flight]
        at = i % flight * PAD
        tail = jnp.where((lane == 2 * i) | (lane == 2 * i + 1), part, 0.0)
        out_ref[at : at + PAD, out_ref.shape[1] - LANES :] = tail.astype(out_ref.dtype)


def add_kernel(flight, keep_ref, got_ref, mix_ref, *outs):
    main = keep_ref.shape[1] - LANES
    for s in range(flight):
        rows = pl.ds(s * PAD, PAD)
        total = keep_ref[rows] + got_ref[rows].astype(F32)
        outs[s][:, :main] = total[:, :main].astype(BF)
        high, low = split(jnp.sum(total[:, main:], axis=1, keepdims=True))
        lane = lax.broadcasted_iota(jnp.int32, (PAD, LANES), 1)
        tail = jnp.where(lane == 0, high.astype(F32), jnp.where(lane == 1, low.astype(F32), 0.0))
        outs[s][:, main : main + LANES] = tail.astype(BF)
    outs[0][:, main + LANES :] = mix_ref[...]


def mix_kernel(flight, ids_ref, place_ref, *refs):
    blocks, (out_ref, gates_ref) = refs[:flight], refs[flight:]
    count, width = out_ref.shape
    main = width * CAP // PAD
    step = width - main
    tn = (((0,), (0,)), ((), ()))
    base = main + LANES
    left = jnp.concatenate(
        [
            blocks[0][:, base + (2 * s + i) * count : base + (2 * s + i + 1) * count]
            for i in range(2)
            for s in range(flight)
        ],
        axis=0,
    )

    def blend(rows):
        right = jnp.concatenate([rows, rows], axis=0)
        return lax.dot_general(left, right, tn, preferred_element_type=F32).astype(BF)

    out_ref[:, :main] = blend(jnp.concatenate([b[:, :main] for b in blocks], axis=0))
    zero = jnp.zeros((PAD - CAP, step), BF)
    folded = []
    for s in range(flight):
        for j in range(main // step):
            folded.append(blocks[s][CAP:, j * step : (j + 1) * step])
        folded.append(zero)
    out_ref[:, main:] = blend(jnp.concatenate(folded, axis=0))
    own = lax.axis_index("expert") // SLICES
    ids = ids_ref[...]
    total = jnp.zeros(ids.shape, F32)
    for s in range(flight):
        q = jnp.sum(blocks[s][:, main:base].astype(F32), axis=1, keepdims=True)
        back = jnp.sum(place_ref[s * PAD : (s + 1) * PAD] * q, axis=0, keepdims=True)
        total = total + jnp.where(ids == (own ^ s), back, 0.0)
    gates_ref[...] = total


def moved(value, sections, devices, stage, flip, bits, only=None):
    route = []
    for p in range(sections):
        for e in range(devices):
            if only is not None and e % 2 != only:
                continue
            route.append((p * devices + e, (p + flip) % sections * devices + (e ^ bits)))
    return lax.ppermute(value, stage, route)


def per_device(inputs, out_grads, expert_ids, gate_values, w_gate, w_up, w_down):
    devices = lax.axis_size("expert")
    sections = lax.axis_size("pipe")
    flight = devices // SLICES
    count, width = inputs.shape[1:]
    axes = ("pipe", "expert")
    go = functools.partial(moved, sections=sections, devices=devices, stage=axes)
    ids = expert_ids[0].T
    gates = gate_values[0].T
    hidden = w_gate.shape[2]
    args = (ids, gates, inputs[0], out_grads[0], w_gate[0], w_up[0], w_down[0])
    shape = jax.ShapeDtypeStruct
    main = width * CAP // PAD
    *blocks, mix, place, pack = pl.pallas_call(
        functools.partial(select_kernel, flight),
        out_shape=[shape((2 * CAP, width), BF)] * flight
        + [shape((PAD, 2 * flight * count), BF), shape((flight * PAD, count), F32)]
        + [shape((3 * width, hidden), BF)],
        in_specs=[pl.BlockSpec(memory_space=pltpu.HBM)] * 7,
        scratch_shapes=[
            pltpu.VMEM(ids.shape, jnp.int32),
            pltpu.VMEM(gates.shape, F32),
            pltpu.VMEM((count, width), BF),
            pltpu.VMEM((count, width), BF),
            pltpu.SemaphoreType.DMA((6 + width // hidden,)),
        ],
        compiler_params=PARAMS,
        name="select",
    )(*[pltpu.with_memory_space_constraint(v, pltpu.HBM) for v in args])
    near = go(pack, flip=0, bits=1)
    rows = [blocks[0]] + [go(blocks[s], flip=0, bits=SLICES * s) for s in range(1, flight)]
    across = [go(rows[0], flip=0, bits=2)]
    rows[-1], near = lax.optimization_barrier((rows[-1], near))
    rows = rows + across + [go(r, flip=0, bits=2) for r in rows[1:]]
    left, part = pl.pallas_call(
        functools.partial(hidden_kernel, flight),
        out_shape=[shape((2 * flight * CAP, 4 * hidden), BF), shape((PAD, LANES), BF)],
        compiler_params=PARAMS,
        name="hidden",
    )(*rows, pack, near)
    part = go(part, flip=1, bits=0)
    r_shapes = [shape((flight * PAD, main + LANES), t) for t in (F32, BF)]
    r_keep, r_send = pl.pallas_call(
        functools.partial(inputs_kernel, flight),
        out_shape=r_shapes,
        compiler_params=PARAMS,
        name="inputs_back",
    )(left, pack, near)
    r_keep, r_send = pl.pallas_call(
        functools.partial(attach_kernel, flight),
        out_shape=r_shapes,
        input_output_aliases={1: 0, 2: 1},
        compiler_params=PARAMS,
        name="attach_gate_parts",
    )(part, r_keep, r_send)
    r_got = go(r_send, flip=0, bits=2)
    extra = 2 * flight * count
    r_parts = pl.pallas_call(
        functools.partial(add_kernel, flight),
        out_shape=[shape((PAD, main + LANES + (extra if s == 0 else 0)), BF) for s in range(flight)],
        compiler_params=PARAMS,
        name="add_inputs_back",
    )(r_keep, r_got, mix)
    r_home = [go(r_parts[s], flip=-1, bits=SLICES * s) for s in range(flight)]
    moe, d_gates = pl.pallas_call(
        functools.partial(mix_kernel, flight),
        out_shape=[shape((count, width), BF), shape(ids.shape, F32)],
        compiler_params=PARAMS,
        name="mix",
    )(ids, place, *r_home)
    return (moe[None], d_gates.T[None])


def solution(mesh):
    return jax.shard_map(
        per_device,
        mesh=mesh,
        in_specs=(
            P("pipe", "expert", None),
            P("pipe", "expert", None),
            P("pipe", "expert", None),
            P("pipe", "expert", None),
            P("pipe", None, "expert"),
            P("pipe", None, "expert"),
            P("pipe", "expert", None),
        ),
        out_specs=(P("pipe", "expert", None), P("pipe", "expert", None)),
        check_vma=False,
    )
```

```python
import functools

import jax
import jax.numpy as jnp
from jax import lax
from jax.experimental import pallas as pl
from jax.experimental.pallas import tpu as pltpu
from jax.sharding import PartitionSpec as P

SLICES = 4
CAP = 12
PAD = 16
LANES = 128
BF = jnp.bfloat16
F32 = jnp.float32
PARAMS = pltpu.CompilerParams(vmem_limit_bytes=40 * 1024 * 1024)


def split(value):
    high = value.astype(BF)
    return high, (value - high.astype(F32)).astype(BF)


def weight_copies(wg_hbm, wu_hbm, wd_hbm, pack_ref, sems):
    width, hidden = wg_hbm.shape
    copies = [
        pltpu.make_async_copy(wg_hbm, pack_ref.at[pl.ds(0, width)], sems.at[0]),
        pltpu.make_async_copy(wu_hbm, pack_ref.at[pl.ds(width, width)], sems.at[1]),
    ]
    for k in range(width // hidden):
        part = pack_ref.at[pl.ds(2 * width + k * hidden, hidden)]
        copies.append(pltpu.make_async_copy(wd_hbm.at[:, pl.ds(k * hidden, hidden)], part, sems.at[2 + k]))
    return copies


def select_kernel(flight, ids_hbm, gates_hbm, x_hbm, g_hbm, wg_hbm, wu_hbm, wd_hbm, *refs):
    blocks, (mix_ref, place_ref, pack_ref) = refs[:flight], refs[flight : flight + 3]
    ids_ref, gates_ref, x_ref, g_ref, sems, pack_sems = refs[flight + 3 :]
    later = weight_copies(wg_hbm, wu_hbm, wd_hbm, pack_ref, pack_sems)
    first = [
        pltpu.make_async_copy(src, dst, sems.at[i])
        for i, (src, dst) in enumerate(
            [(ids_hbm, ids_ref), (gates_hbm, gates_ref), (x_hbm, x_ref), (g_hbm, g_ref)]
        )
    ]
    for copy in first + later:
        copy.start()
    own = lax.axis_index("expert") // SLICES
    parity = lax.axis_index("expert") % 2
    first[0].wait()
    first[1].wait()
    ids = ids_ref[...]
    gates = gates_ref[...]
    count = ids.shape[1]
    routed, weight = [], []
    for s in range(flight):
        match = ids == (own ^ s ^ parity)
        routed.append(jnp.sum(jnp.where(match, 1.0, 0.0), axis=0, keepdims=True))
        weight.append(jnp.sum(jnp.where(match, gates, 0.0), axis=0, keepdims=True))
    fill = [jnp.zeros((1, count), F32)] * (-flight % 8)
    table = jnp.concatenate(routed + fill, axis=0)
    earlier = lax.broadcasted_iota(jnp.int32, (count, count), 0) < lax.broadcasted_iota(
        jnp.int32, (count, count), 1
    )
    rank = jnp.dot(
        table.astype(BF), jnp.where(earlier, 1.0, 0.0).astype(BF), preferred_element_type=F32
    )
    key = jnp.where((table > 0.0) & (rank < float(CAP)), rank, -1.0)
    row = lax.broadcasted_iota(jnp.int32, (2 * CAP, count), 0)
    is_x = row < CAP
    slot = jnp.where(is_x, row, row - CAP).astype(F32)
    slot16 = lax.broadcasted_iota(jnp.int32, (PAD, count), 0)
    slot16 = jnp.where(slot16 < CAP, slot16, -2).astype(F32)
    picks_x, picks_g = [], []
    for s in [*range(0, flight, 2), *range(1, flight, 2)]:
        hit = key[s : s + 1] == slot
        picks_x.append(jnp.where(hit & is_x, 1.0, 0.0))
        picks_g.append(jnp.where(hit & ~is_x, 1.0, 0.0))
        at = jnp.where(key[s : s + 1] == slot16, 1.0, 0.0)
        place_ref[s * PAD : (s + 1) * PAD] = at
        for i, value in enumerate(split(at * weight[s])):
            mix_ref[:, (2 * s + i) * count : (2 * s + i + 1) * count] = value
    pick_x = jnp.concatenate(picks_x, axis=0).astype(BF)
    pick_g = jnp.concatenate(picks_g, axis=0).astype(BF)
    first[2].wait()
    rows = jnp.dot(pick_x, x_ref[...], preferred_element_type=F32)
    first[3].wait()
    rows = rows + jnp.dot(pick_g, g_ref[...], preferred_element_type=F32)
    rows = rows.astype(BF)
    for i in range(flight):
        blocks[i][...] = rows[i * 2 * CAP : (i + 1) * 2 * CAP]
    for copy in later:
        copy.wait()


def join_kernel(mine_ref, got_ref, out_ref):
    out_ref[: 2 * CAP] = mine_ref[...]
    out_ref[2 * CAP :] = got_ref[...]


def hidden_kernel(many, *refs):
    blocks, packs = refs[:many], refs[many : many + 2]
    left_ref, part_ref = refs[many + 2 :]
    step = 2 * CAP
    spots = [(b, at) for b in blocks for at in range(0, b.shape[0], step)]
    x = jnp.concatenate([b[at : at + CAP] for b, at in spots], axis=0)
    g = jnp.concatenate([b[at + CAP : at + step] for b, at in spots], axis=0)
    width = x.shape[1]
    hidden = packs[0].shape[1]
    nt = (((1,), (1,)), ((), ()))
    part = jnp.zeros((x.shape[0], 1), F32)
    for half, pack in enumerate(packs):
        a = jnp.dot(x, pack[:width], preferred_element_type=F32)
        u = jnp.dot(x, pack[width : 2 * width], preferred_element_type=F32)
        dh = jnp.zeros_like(a)
        for k in range(0, width, hidden):
            down = pack[2 * width + k : 2 * width + k + hidden]
            dh = dh + lax.dot_general(g[:, k : k + hidden], down, nt, preferred_element_type=F32)
        sig = jax.nn.sigmoid(a)
        act = a * sig
        part = part + jnp.sum(act * u * dh, axis=1, keepdims=True)
        at = 2 * half * hidden
        left_ref[:, at : at + hidden] = (dh * u * sig * (1.0 + a * (1.0 - sig))).astype(BF)
        left_ref[:, at + hidden : at + 2 * hidden] = (dh * act).astype(BF)
    high, low = split(part)
    high, low = high.astype(F32), low.astype(F32)
    lane = lax.broadcasted_iota(jnp.int32, (CAP, LANES), 1)
    tail = jnp.zeros((CAP, LANES), F32)
    for i in range(len(spots)):
        rows = slice(i * CAP, (i + 1) * CAP)
        tail = jnp.where(lane == 2 * i, high[rows], jnp.where(lane == 2 * i + 1, low[rows], tail))
    part_ref[...] = jnp.concatenate([tail, jnp.zeros((PAD - CAP, LANES), F32)], axis=0).astype(BF)


def inputs_kernel(left_ref, own_ref, near_ref, *outs):
    hidden = own_ref.shape[1]
    width = own_ref.shape[0] // 3
    nt = (((1,), (1,)), ((), ()))
    main = width * CAP // PAD
    step = width - main
    extra = PAD - CAP
    pieces = []
    for c in range(0, width, step):
        total = jnp.zeros((left_ref.shape[0], step), F32)
        for i in range(4):
            pack = (own_ref, near_ref)[i // 2]
            right = pack[i % 2 * width + c : i % 2 * width + c + step]
            left = left_ref[:, i * hidden : (i + 1) * hidden]
            total = total + lax.dot_general(left, right, nt, preferred_element_type=F32)
        pieces.append(total)
    last = pieces[-1]
    each = outs[0].shape[0] // PAD
    for i in range(left_ref.shape[0] // CAP):
        base = i * CAP
        out_ref, at = outs[i // each], i % each * PAD
        for j, piece in enumerate(pieces[:-1]):
            under = last[base + extra * j : base + extra * (j + 1)]
            both = jnp.concatenate([piece[base : base + CAP], under], axis=0)
            out_ref[at : at + PAD, j * step : (j + 1) * step] = both.astype(out_ref.dtype)


def attach_kernel(part_ref, *refs):
    outs = refs[len(refs) // 2 :]
    part = part_ref[...].astype(F32)
    lane = lax.broadcasted_iota(jnp.int32, part.shape, 1)
    each = outs[0].shape[0] // PAD
    for i in range(len(outs) * each):
        out_ref, at = outs[i // each], i % each * PAD
        tail = jnp.where(lane // 2 == i, part, 0.0)
        out_ref[at : at + PAD, out_ref.shape[1] - LANES :] = tail.astype(out_ref.dtype)


def add_kernel(keep_ref, got_ref, out_ref):
    main = keep_ref.shape[1] - LANES
    lane = lax.broadcasted_iota(jnp.int32, (PAD, LANES), 1)
    for i in range(2):
        rows = pl.ds(i * PAD, PAD)
        total = keep_ref[rows] + got_ref[rows].astype(F32)
        out_ref[rows, :main] = total[:, :main].astype(BF)
        high, low = split(jnp.sum(total[:, main:], axis=1, keepdims=True))
        tail = jnp.where(lane == 0, high.astype(F32), jnp.where(lane == 1, low.astype(F32), 0.0))
        out_ref[rows, main:] = tail.astype(BF)


def stack_kernel(*refs):
    for k, ref in enumerate(refs[:-1]):
        refs[-1][k * 2 * CAP : (k + 1) * 2 * CAP] = ref[...]


def unstack_kernel(ref, *outs):
    for k, out in enumerate(outs):
        out[...] = ref[k * 2 * CAP : (k + 1) * 2 * CAP]


def other_kernel(*refs):
    half = len(refs) - 1
    for k, ref in zip(reversed(range(half)), refs):
        refs[-1][k * PAD : (k + 1) * PAD] = ref[PAD:]


def mix_kernel(flight, ids_ref, place_ref, mix_ref, near_ref, *refs):
    half = flight // 2
    home, (out_ref, gates_ref) = refs[:half], refs[half:]
    home = home[::-1]
    blocks = []
    for k in range(half):
        blocks += [home[k].at[pl.ds(0, PAD)], near_ref.at[pl.ds(k * PAD, PAD)]]
    count, width = out_ref.shape
    main = width * CAP // PAD
    step = width - main
    tn = (((0,), (0,)), ((), ()))
    left = jnp.concatenate(
        [
            mix_ref[:, (2 * s + i) * count : (2 * s + i + 1) * count]
            for i in range(2)
            for s in range(flight)
        ],
        axis=0,
    )

    def blend(rows):
        right = jnp.concatenate([rows, rows], axis=0)
        return lax.dot_general(left, right, tn, preferred_element_type=F32).astype(BF)

    out_ref[:, :main] = blend(jnp.concatenate([b[:, :main] for b in blocks], axis=0))
    zero = jnp.zeros((PAD - CAP, step), BF)
    folded = []
    for s in range(flight):
        for j in range(main // step):
            folded.append(blocks[s][CAP:, j * step : (j + 1) * step])
        folded.append(zero)
    out_ref[:, main:] = blend(jnp.concatenate(folded, axis=0))
    own = lax.axis_index("expert") // SLICES
    parity = lax.axis_index("expert") % 2
    ids = ids_ref[...]
    total = jnp.zeros(ids.shape, F32)
    for s in range(flight):
        q = jnp.sum(blocks[s][:, main:].astype(F32), axis=1, keepdims=True)
        back = jnp.sum(place_ref[s * PAD : (s + 1) * PAD] * q, axis=0, keepdims=True)
        total = total + jnp.where(ids == (own ^ s ^ parity), back, 0.0)
    gates_ref[...] = total


def moved(value, sections, devices, stage, flip, bits, along=0):
    route = []
    for p in range(sections):
        for e in range(devices):
            there = e ^ bits ^ (along + SLICES * (e % 2) if along is not None else 0)
            route.append((p * devices + e, (p + flip) % sections * devices + there))
    return lax.ppermute(value, stage, route)


def per_device(inputs, out_grads, expert_ids, gate_values, w_gate, w_up, w_down):
    devices = lax.axis_size("expert")
    sections = lax.axis_size("pipe")
    flight = devices // SLICES
    half = flight // 2
    count, width = inputs.shape[1:]
    go = functools.partial(moved, sections=sections, devices=devices, stage=("pipe", "expert"))
    ids = expert_ids[0].T
    gates = gate_values[0].T
    hidden = w_gate.shape[2]
    shape = jax.ShapeDtypeStruct
    main = width * CAP // PAD
    hbm = [pl.BlockSpec(memory_space=pltpu.HBM)]
    args = (ids, gates, inputs[0], out_grads[0], w_gate[0], w_up[0], w_down[0])
    *blocks, mix, place, pack = pl.pallas_call(
        functools.partial(select_kernel, flight),
        out_shape=[shape((2 * CAP, width), BF)] * flight
        + [
            shape((PAD, 2 * flight * count), BF),
            shape((flight * PAD, count), F32),
            shape((3 * width, hidden), BF),
        ],
        in_specs=hbm * 7,
        scratch_shapes=[
            pltpu.VMEM(ids.shape, jnp.int32),
            pltpu.VMEM(gates.shape, F32),
            pltpu.VMEM((count, width), BF),
            pltpu.VMEM((count, width), BF),
            pltpu.SemaphoreType.DMA((4,)),
            pltpu.SemaphoreType.DMA((2 + width // hidden,)),
        ],
        compiler_params=PARAMS,
        name="select",
    )(*[pltpu.with_memory_space_constraint(v, pltpu.HBM) for v in args])
    mine, theirs = blocks[:half], blocks[half:]
    both = pl.pallas_call(
        stack_kernel,
        out_shape=shape((half * 2 * CAP, width), BF),
        compiler_params=PARAMS,
        name="stack",
    )(*theirs)
    both = go(both, flip=0, bits=1, along=None)
    got = pl.pallas_call(
        unstack_kernel,
        out_shape=[shape((2 * CAP, width), BF)] * half,
        compiler_params=PARAMS,
        name="unstack",
    )(both)
    joined = pl.pallas_call(
        join_kernel,
        out_shape=shape((4 * CAP, width), BF),
        compiler_params=PARAMS,
        name="join",
    )(mine[0], got[0])
    sends = [(0, joined)]
    for k in range(1, half):
        sends += [(k, mine[k]), (k, got[k])]
    rows = [go(v, flip=0, bits=0, along=2 * k * SLICES) for k, v in sends]
    far_mix = go(mix, flip=-1, bits=0, along=None)
    rows[-1], far_mix = lax.optimization_barrier((rows[-1], far_mix))
    pack, *_ = lax.optimization_barrier((pack, *got))
    near = go(pack, flip=0, bits=1, along=None)
    rows = rows + [go(r, flip=0, bits=2, along=None) for r in rows]
    left, part = pl.pallas_call(
        functools.partial(hidden_kernel, len(rows)),
        out_shape=[shape((2 * flight * CAP, 4 * hidden), BF), shape((PAD, LANES), BF)],
        compiler_params=PARAMS,
        name="hidden",
    )(*rows, pack, near)
    part = go(part, flip=1, bits=0, along=None)
    r_shapes = [shape((2 * PAD, main + LANES), t) for t in [F32] * half + [BF] * half]
    r_sums = pl.pallas_call(
        inputs_kernel,
        out_shape=r_shapes,
        compiler_params=PARAMS,
        name="inputs_back",
    )(left, pack, near)
    r_sums = pl.pallas_call(
        attach_kernel,
        out_shape=r_shapes,
        input_output_aliases={i + 1: i for i in range(2 * half)},
        compiler_params=PARAMS,
        name="attach_gate_parts",
    )(part, *r_sums)
    r_home = []
    for k in reversed(range(half)):
        r_got = go(r_sums[half + k], flip=0, bits=2, along=None)
        r_part = pl.pallas_call(
            add_kernel,
            out_shape=shape((2 * PAD, main + LANES), BF),
            compiler_params=PARAMS,
            name="add_inputs_back",
        )(r_sums[k], r_got)
        r_home.append(go(r_part, flip=-1, bits=0, along=2 * k * SLICES))
    others = pl.pallas_call(
        other_kernel,
        out_shape=shape((half * PAD, main + LANES), BF),
        compiler_params=PARAMS,
        name="other_core",
    )(*r_home)
    r_near = go(others, flip=0, bits=1, along=None)
    moe, d_gates = pl.pallas_call(
        functools.partial(mix_kernel, flight),
        out_shape=[shape((count, width), BF), shape(ids.shape, F32)],
        compiler_params=PARAMS,
        name="mix",
    )(ids, place, far_mix, r_near, *r_home)
    return (moe[None], d_gates.T[None])


def solution(mesh):
    return jax.shard_map(
        per_device,
        mesh=mesh,
        in_specs=(
            P("pipe", "expert", None),
            P("pipe", "expert", None),
            P("pipe", "expert", None),
            P("pipe", "expert", None),
            P("pipe", None, "expert"),
            P("pipe", None, "expert"),
            P("pipe", "expert", None),
        ),
        out_specs=(P("pipe", "expert", None), P("pipe", "expert", None)),
        check_vma=False,
    )
```

```python
import functools

import jax
import jax.numpy as jnp
from jax import lax
from jax.experimental import pallas as pl
from jax.experimental.pallas import tpu as pltpu
from jax.sharding import PartitionSpec as P

SLICES = 4
CAP = 12
PAD = 16
LANES = 128
ORDER = ((1, 3, 2, 0), (1, 0, 3, 2))
BF = jnp.bfloat16
F32 = jnp.float32
PARAMS = pltpu.CompilerParams(vmem_limit_bytes=40 * 1024 * 1024)


def split(value):
    high = value.astype(BF)
    return high, (value - high.astype(F32)).astype(BF)


def weight_copies(wg_hbm, wu_hbm, wd_hbm, pack_ref, sems):
    width, hidden = wg_hbm.shape
    copies = [
        pltpu.make_async_copy(wg_hbm, pack_ref.at[pl.ds(0, width)], sems.at[0]),
        pltpu.make_async_copy(wu_hbm, pack_ref.at[pl.ds(width, width)], sems.at[1]),
    ]
    for k in range(width // hidden):
        part = pack_ref.at[pl.ds(2 * width + k * hidden, hidden)]
        copies.append(pltpu.make_async_copy(wd_hbm.at[:, pl.ds(k * hidden, hidden)], part, sems.at[2 + k]))
    return copies


def select_kernel(flight, ids_hbm, gates_hbm, x_hbm, g_hbm, wg_hbm, wu_hbm, wd_hbm, *refs):
    blocks, (mix_ref, place_ref, pack_ref) = refs[:flight], refs[flight : flight + 3]
    ids_ref, gates_ref, x_ref, g_ref, sems, pack_sems = refs[flight + 3 :]
    later = weight_copies(wg_hbm, wu_hbm, wd_hbm, pack_ref, pack_sems)
    first = [
        pltpu.make_async_copy(src, dst, sems.at[i])
        for i, (src, dst) in enumerate(
            [(ids_hbm, ids_ref), (gates_hbm, gates_ref), (x_hbm, x_ref), (g_hbm, g_ref)]
        )
    ]
    for copy in first + later:
        copy.start()
    own = lax.axis_index("expert") // SLICES
    parity = lax.axis_index("expert") % 2
    first[0].wait()
    first[1].wait()
    ids = ids_ref[...]
    gates = gates_ref[...]
    count = ids.shape[1]
    routed, weight = [], []
    for s in range(flight):
        match = ids == (own ^ s ^ parity)
        routed.append(jnp.sum(jnp.where(match, 1.0, 0.0), axis=0, keepdims=True))
        weight.append(jnp.sum(jnp.where(match, gates, 0.0), axis=0, keepdims=True))
    fill = [jnp.zeros((1, count), F32)] * (-flight % 8)
    table = jnp.concatenate(routed + fill, axis=0)
    earlier = lax.broadcasted_iota(jnp.int32, (count, count), 0) < lax.broadcasted_iota(
        jnp.int32, (count, count), 1
    )
    rank = jnp.dot(
        table.astype(BF), jnp.where(earlier, 1.0, 0.0).astype(BF), preferred_element_type=F32
    )
    key = jnp.where((table > 0.0) & (rank < float(CAP)), rank, -1.0)
    row = lax.broadcasted_iota(jnp.int32, (2 * CAP, count), 0)
    is_x = row < CAP
    slot = jnp.where(is_x, row, row - CAP).astype(F32)
    slot16 = lax.broadcasted_iota(jnp.int32, (PAD, count), 0)
    slot16 = jnp.where(slot16 < CAP, slot16, -2).astype(F32)
    picks_x, picks_g = [], []
    for s in [*range(0, flight, 2), *range(1, flight, 2)]:
        hit = key[s : s + 1] == slot
        picks_x.append(jnp.where(hit & is_x, 1.0, 0.0))
        picks_g.append(jnp.where(hit & ~is_x, 1.0, 0.0))
        at = jnp.where(key[s : s + 1] == slot16, 1.0, 0.0)
        place_ref[s * PAD : (s + 1) * PAD] = at
        for i, value in enumerate(split(at * weight[s])):
            mix_ref[:, (2 * s + i) * count : (2 * s + i + 1) * count] = value
    pick_x = jnp.concatenate(picks_x, axis=0).astype(BF)
    pick_g = jnp.concatenate(picks_g, axis=0).astype(BF)
    first[2].wait()
    rows = jnp.dot(pick_x, x_ref[...], preferred_element_type=F32)
    first[3].wait()
    rows = rows + jnp.dot(pick_g, g_ref[...], preferred_element_type=F32)
    rows = rows.astype(BF)
    for i in range(flight):
        blocks[i][...] = rows[i * 2 * CAP : (i + 1) * 2 * CAP]
    for copy in later:
        copy.wait()


def hidden_kernel(order, *refs):
    many = len(order)
    blocks, packs = refs[:many], refs[many : many + 2]
    left_ref, part_ref = refs[many + 2 :]
    blocks = [blocks[order.index(i)] for i in range(many)]
    step = 2 * CAP
    spots = [(b, at) for b in blocks for at in range(0, b.shape[0], step)]
    x = jnp.concatenate([b[at : at + CAP] for b, at in spots], axis=0)
    g = jnp.concatenate([b[at + CAP : at + step] for b, at in spots], axis=0)
    width = x.shape[1]
    hidden = packs[0].shape[1]
    nt = (((1,), (1,)), ((), ()))
    part = jnp.zeros((x.shape[0], 1), F32)
    for half, pack in enumerate(packs):
        a = jnp.dot(x, pack[:width], preferred_element_type=F32)
        u = jnp.dot(x, pack[width : 2 * width], preferred_element_type=F32)
        dh = jnp.zeros_like(a)
        for k in range(0, width, hidden):
            down = pack[2 * width + k : 2 * width + k + hidden]
            dh = dh + lax.dot_general(g[:, k : k + hidden], down, nt, preferred_element_type=F32)
        sig = jax.nn.sigmoid(a)
        act = a * sig
        part = part + jnp.sum(act * u * dh, axis=1, keepdims=True)
        at = 2 * half * hidden
        left_ref[:, at : at + hidden] = (dh * u * sig * (1.0 + a * (1.0 - sig))).astype(BF)
        left_ref[:, at + hidden : at + 2 * hidden] = (dh * act).astype(BF)
    high, low = split(part)
    high, low = high.astype(F32), low.astype(F32)
    lane = lax.broadcasted_iota(jnp.int32, (CAP, LANES), 1)
    tail = jnp.zeros((CAP, LANES), F32)
    for i in range(len(spots)):
        rows = slice(i * CAP, (i + 1) * CAP)
        tail = jnp.where(lane == 2 * i, high[rows], jnp.where(lane == 2 * i + 1, low[rows], tail))
    part_ref[...] = jnp.concatenate([tail, jnp.zeros((PAD - CAP, LANES), F32)], axis=0).astype(BF)


def inputs_kernel(left_ref, own_ref, near_ref, *outs):
    hidden = own_ref.shape[1]
    width = own_ref.shape[0] // 3
    nt = (((1,), (1,)), ((), ()))
    main = width * CAP // PAD
    step = width - main
    extra = PAD - CAP
    pieces = []
    for c in range(0, width, step):
        total = jnp.zeros((left_ref.shape[0], step), F32)
        for i in range(4):
            pack = (own_ref, near_ref)[i // 2]
            right = pack[i % 2 * width + c : i % 2 * width + c + step]
            left = left_ref[:, i * hidden : (i + 1) * hidden]
            total = total + lax.dot_general(left, right, nt, preferred_element_type=F32)
        pieces.append(total)
    last = pieces[-1]
    each = outs[0].shape[0] // PAD
    for i in range(left_ref.shape[0] // CAP):
        base = i * CAP
        out_ref, at = outs[i // each], i % each * PAD
        for j, piece in enumerate(pieces[:-1]):
            under = last[base + extra * j : base + extra * (j + 1)]
            both = jnp.concatenate([piece[base : base + CAP], under], axis=0)
            out_ref[at : at + PAD, j * step : (j + 1) * step] = both.astype(out_ref.dtype)


def attach_kernel(part_ref, *refs):
    outs = refs[len(refs) // 2 :]
    part = part_ref[...].astype(F32)
    lane = lax.broadcasted_iota(jnp.int32, part.shape, 1)
    each = outs[0].shape[0] // PAD
    for i in range(len(outs) * each):
        out_ref, at = outs[i // each], i % each * PAD
        tail = jnp.where(lane // 2 == i, part, 0.0)
        out_ref[at : at + PAD, out_ref.shape[1] - LANES :] = tail.astype(out_ref.dtype)


def add_kernel(keep_ref, got_ref, out_ref):
    main = keep_ref.shape[1] - LANES
    lane = lax.broadcasted_iota(jnp.int32, (PAD, LANES), 1)
    for i in range(2):
        rows = pl.ds(i * PAD, PAD)
        total = keep_ref[rows] + got_ref[rows].astype(F32)
        out_ref[rows, :main] = total[:, :main].astype(BF)
        high, low = split(jnp.sum(total[:, main:], axis=1, keepdims=True))
        tail = jnp.where(lane == 0, high.astype(F32), jnp.where(lane == 1, low.astype(F32), 0.0))
        out_ref[rows, main:] = tail.astype(BF)


def other_kernel(*refs):
    half = len(refs) - 1
    for k, ref in zip(reversed(range(half)), refs):
        refs[-1][k * PAD : (k + 1) * PAD] = ref[PAD:]


def mix_kernel(flight, ids_ref, place_ref, mix_ref, near_ref, *refs):
    half = flight // 2
    home, (out_ref, gates_ref) = refs[:half], refs[half:]
    home = home[::-1]
    blocks = []
    for k in range(half):
        blocks += [home[k].at[pl.ds(0, PAD)], near_ref.at[pl.ds(k * PAD, PAD)]]
    count, width = out_ref.shape
    main = width * CAP // PAD
    step = width - main
    tn = (((0,), (0,)), ((), ()))
    left = jnp.concatenate(
        [
            mix_ref[:, (2 * s + i) * count : (2 * s + i + 1) * count]
            for i in range(2)
            for s in range(flight)
        ],
        axis=0,
    )

    def blend(rows):
        right = jnp.concatenate([rows, rows], axis=0)
        return lax.dot_general(left, right, tn, preferred_element_type=F32).astype(BF)

    out_ref[:, :main] = blend(jnp.concatenate([b[:, :main] for b in blocks], axis=0))
    zero = jnp.zeros((PAD - CAP, step), BF)
    folded = []
    for s in range(flight):
        for j in range(main // step):
            folded.append(blocks[s][CAP:, j * step : (j + 1) * step])
        folded.append(zero)
    out_ref[:, main:] = blend(jnp.concatenate(folded, axis=0))
    own = lax.axis_index("expert") // SLICES
    parity = lax.axis_index("expert") % 2
    ids = ids_ref[...]
    total = jnp.zeros(ids.shape, F32)
    for s in range(flight):
        q = jnp.sum(blocks[s][:, main:].astype(F32), axis=1, keepdims=True)
        back = jnp.sum(place_ref[s * PAD : (s + 1) * PAD] * q, axis=0, keepdims=True)
        total = total + jnp.where(ids == (own ^ s ^ parity), back, 0.0)
    gates_ref[...] = total


def moved(value, sections, devices, stage, flip, bits, along=0):
    route = []
    for p in range(sections):
        for e in range(devices):
            there = e ^ bits ^ (along + SLICES * ((e ^ bits) % 2) if along is not None else 0)
            route.append((p * devices + e, (p + flip) % sections * devices + there))
    return lax.ppermute(value, stage, route)


def per_device(inputs, out_grads, expert_ids, gate_values, w_gate, w_up, w_down):
    devices = lax.axis_size("expert")
    sections = lax.axis_size("pipe")
    flight = devices // SLICES
    half = flight // 2
    count, width = inputs.shape[1:]
    go = functools.partial(moved, sections=sections, devices=devices, stage=("pipe", "expert"))
    ids = expert_ids[0].T
    gates = gate_values[0].T
    hidden = w_gate.shape[2]
    shape = jax.ShapeDtypeStruct
    main = width * CAP // PAD
    hbm = [pl.BlockSpec(memory_space=pltpu.HBM)]
    args = (ids, gates, inputs[0], out_grads[0], w_gate[0], w_up[0], w_down[0])
    *blocks, mix, place, pack = pl.pallas_call(
        functools.partial(select_kernel, flight),
        out_shape=[shape((2 * CAP, width), BF)] * flight
        + [
            shape((PAD, 2 * flight * count), BF),
            shape((flight * PAD, count), F32),
            shape((3 * width, hidden), BF),
        ],
        in_specs=hbm * 7,
        scratch_shapes=[
            pltpu.VMEM(ids.shape, jnp.int32),
            pltpu.VMEM(gates.shape, F32),
            pltpu.VMEM((count, width), BF),
            pltpu.VMEM((count, width), BF),
            pltpu.SemaphoreType.DMA((4,)),
            pltpu.SemaphoreType.DMA((2 + width // hidden,)),
        ],
        compiler_params=PARAMS,
        name="select",
    )(*[pltpu.with_memory_space_constraint(v, pltpu.HBM) for v in args])
    mine, theirs = blocks[:half], blocks[half:]
    rows = []
    for k in range(half):
        rows.append(go(mine[k], flip=0, bits=0, along=2 * k * SLICES))
        rows.append(go(theirs[k], flip=0, bits=1, along=2 * k * SLICES))
    near = go(pack, flip=0, bits=1, along=None)
    rows[-1], near = lax.optimization_barrier((rows[-1], near))
    rows = rows + [go(r, flip=0, bits=2, along=None) for r in rows]
    order = [*ORDER[0], *range(4, flight), *(flight + i for i in ORDER[1]), *range(flight + 4, 2 * flight)]
    left, part = pl.pallas_call(
        functools.partial(hidden_kernel, order),
        out_shape=[shape((2 * flight * CAP, 4 * hidden), BF), shape((PAD, LANES), BF)],
        compiler_params=PARAMS,
        name="hidden",
    )(*[rows[i] for i in order], pack, near)
    part = go(part, flip=1, bits=0, along=None)
    r_shapes = [shape((2 * PAD, main + LANES), t) for t in [F32] * half + [BF] * half]
    r_sums = pl.pallas_call(
        inputs_kernel,
        out_shape=r_shapes,
        compiler_params=PARAMS,
        name="inputs_back",
    )(left, pack, near)
    r_sums = pl.pallas_call(
        attach_kernel,
        out_shape=r_shapes,
        input_output_aliases={i + 1: i for i in range(2 * half)},
        compiler_params=PARAMS,
        name="attach_gate_parts",
    )(part, *r_sums)
    r_home = []
    for k in range(half):
        r_got = go(r_sums[half + k], flip=0, bits=2, along=None)
        r_part = pl.pallas_call(
            add_kernel,
            out_shape=shape((2 * PAD, main + LANES), BF),
            compiler_params=PARAMS,
            name="add_inputs_back",
        )(r_sums[k], r_got)
        r_home.append(go(r_part, flip=-1, bits=0, along=2 * k * SLICES))
    far_mix = go(mix, flip=-1, bits=0, along=None)
    r_home[-1], far_mix = lax.optimization_barrier((r_home[-1], far_mix))
    others = pl.pallas_call(
        other_kernel,
        out_shape=shape((half * PAD, main + LANES), BF),
        compiler_params=PARAMS,
        name="other_core",
    )(*r_home[::-1])
    r_near = go(others, flip=0, bits=1, along=None)
    moe, d_gates = pl.pallas_call(
        functools.partial(mix_kernel, flight),
        out_shape=[shape((count, width), BF), shape(ids.shape, F32)],
        compiler_params=PARAMS,
        name="mix",
    )(ids, place, far_mix, r_near, *r_home[::-1])
    return (moe[None], d_gates.T[None])


def solution(mesh):
    return jax.shard_map(
        per_device,
        mesh=mesh,
        in_specs=(
            P("pipe", "expert", None),
            P("pipe", "expert", None),
            P("pipe", "expert", None),
            P("pipe", "expert", None),
            P("pipe", None, "expert"),
            P("pipe", None, "expert"),
            P("pipe", "expert", None),
        ),
        out_specs=(P("pipe", "expert", None), P("pipe", "expert", None)),
        check_vma=False,
    )
```

```python
import functools

import jax
import jax.numpy as jnp
from jax import lax
from jax.experimental import pallas as pl
from jax.experimental.pallas import tpu as pltpu
from jax.sharding import PartitionSpec as P

SLICES = 4
CAP = 12
PAD = 16
LANES = 128
ORDER = ((1, 3, 2, 0), (1, 0, 3, 2))
BF = jnp.bfloat16
F32 = jnp.float32
PARAMS = pltpu.CompilerParams(vmem_limit_bytes=40 * 1024 * 1024)


def split(value):
    high = value.astype(BF)
    return high, (value - high.astype(F32)).astype(BF)


def weight_copies(wg_hbm, wu_hbm, wd_hbm, pack_ref, sems):
    width, hidden = wg_hbm.shape
    copies = [
        pltpu.make_async_copy(wg_hbm, pack_ref.at[pl.ds(0, width)], sems.at[0]),
        pltpu.make_async_copy(wu_hbm, pack_ref.at[pl.ds(width, width)], sems.at[1]),
    ]
    for k in range(width // hidden):
        part = pack_ref.at[pl.ds(2 * width + k * hidden, hidden)]
        copies.append(pltpu.make_async_copy(wd_hbm.at[:, pl.ds(k * hidden, hidden)], part, sems.at[2 + k]))
    return copies


def select_kernel(flight, ids_hbm, gates_hbm, x_hbm, g_hbm, wg_hbm, wu_hbm, wd_hbm, *refs):
    blocks, (mix_ref, place_ref, pack_ref) = refs[:flight], refs[flight : flight + 3]
    ids_ref, gates_ref, x_ref, g_ref, sems, pack_sems = refs[flight + 3 :]
    later = weight_copies(wg_hbm, wu_hbm, wd_hbm, pack_ref, pack_sems)
    first = [
        pltpu.make_async_copy(src, dst, sems.at[i])
        for i, (src, dst) in enumerate(
            [(ids_hbm, ids_ref), (gates_hbm, gates_ref), (x_hbm, x_ref), (g_hbm, g_ref)]
        )
    ]
    for copy in first:
        copy.start()
    for copy in later:
        copy.start(priority=1)
    own = lax.axis_index("expert") // SLICES
    parity = lax.axis_index("expert") % 2
    first[0].wait()
    first[1].wait()
    ids = ids_ref[...]
    gates = gates_ref[...]
    count = ids.shape[1]
    routed, weight = [], []
    for s in range(flight):
        match = ids == (own ^ s ^ parity)
        routed.append(jnp.sum(jnp.where(match, 1.0, 0.0), axis=0, keepdims=True))
        weight.append(jnp.sum(jnp.where(match, gates, 0.0), axis=0, keepdims=True))
    fill = [jnp.zeros((1, count), F32)] * (-flight % 8)
    table = jnp.concatenate(routed + fill, axis=0)
    earlier = lax.broadcasted_iota(jnp.int32, (count, count), 0) < lax.broadcasted_iota(
        jnp.int32, (count, count), 1
    )
    rank = jnp.dot(
        table.astype(BF), jnp.where(earlier, 1.0, 0.0).astype(BF), preferred_element_type=F32
    )
    key = jnp.where((table > 0.0) & (rank < float(CAP)), rank, -1.0)
    row = lax.broadcasted_iota(jnp.int32, (2 * CAP, count), 0)
    is_x = row < CAP
    slot = jnp.where(is_x, row, row - CAP).astype(F32)
    slot16 = lax.broadcasted_iota(jnp.int32, (PAD, count), 0)
    slot16 = jnp.where(slot16 < CAP, slot16, -2).astype(F32)
    picks_x, picks_g = [], []
    for s in [*range(0, flight, 2), *range(1, flight, 2)]:
        hit = key[s : s + 1] == slot
        picks_x.append(jnp.where(hit & is_x, 1.0, 0.0))
        picks_g.append(jnp.where(hit & ~is_x, 1.0, 0.0))
        at = jnp.where(key[s : s + 1] == slot16, 1.0, 0.0)
        place_ref[s * PAD : (s + 1) * PAD] = at
        for i, value in enumerate(split(at * weight[s])):
            mix_ref[:, (2 * s + i) * count : (2 * s + i + 1) * count] = value
    pick_x = jnp.concatenate(picks_x, axis=0).astype(BF)
    pick_g = jnp.concatenate(picks_g, axis=0).astype(BF)
    first[2].wait()
    rows = jnp.dot(pick_x, x_ref[...], preferred_element_type=F32)
    first[3].wait()
    rows = rows + jnp.dot(pick_g, g_ref[...], preferred_element_type=F32)
    rows = rows.astype(BF)
    for i in range(flight):
        blocks[i][...] = rows[i * 2 * CAP : (i + 1) * 2 * CAP]
    for copy in later:
        copy.wait()


def hidden_kernel(order, *refs):
    many = len(order)
    blocks, packs = refs[:many], refs[many : many + 2]
    left_ref, part_ref = refs[many + 2 :]
    blocks = [blocks[order.index(i)] for i in range(many)]
    step = 2 * CAP
    spots = [(b, at) for b in blocks for at in range(0, b.shape[0], step)]
    x = jnp.concatenate([b[at : at + CAP] for b, at in spots], axis=0)
    g = jnp.concatenate([b[at + CAP : at + step] for b, at in spots], axis=0)
    width = x.shape[1]
    hidden = packs[0].shape[1]
    nt = (((1,), (1,)), ((), ()))
    part = jnp.zeros((x.shape[0], 1), F32)
    for half, pack in enumerate(packs):
        a = jnp.dot(x, pack[:width], preferred_element_type=F32)
        u = jnp.dot(x, pack[width : 2 * width], preferred_element_type=F32)
        dh = jnp.zeros_like(a)
        for k in range(0, width, hidden):
            down = pack[2 * width + k : 2 * width + k + hidden]
            dh = dh + lax.dot_general(g[:, k : k + hidden], down, nt, preferred_element_type=F32)
        sig = jax.nn.sigmoid(a)
        act = a * sig
        part = part + jnp.sum(act * u * dh, axis=1, keepdims=True)
        at = 2 * half * hidden
        left_ref[:, at : at + hidden] = (dh * u * sig * (1.0 + a * (1.0 - sig))).astype(BF)
        left_ref[:, at + hidden : at + 2 * hidden] = (dh * act).astype(BF)
    high, low = split(part)
    high, low = high.astype(F32), low.astype(F32)
    lane = lax.broadcasted_iota(jnp.int32, (CAP, LANES), 1)
    tail = jnp.zeros((CAP, LANES), F32)
    for i in range(len(spots)):
        rows = slice(i * CAP, (i + 1) * CAP)
        tail = jnp.where(lane == 2 * i, high[rows], jnp.where(lane == 2 * i + 1, low[rows], tail))
    part_ref[...] = jnp.concatenate([tail, jnp.zeros((PAD - CAP, LANES), F32)], axis=0).astype(BF)


def inputs_kernel(left_ref, own_ref, near_ref, *outs):
    hidden = own_ref.shape[1]
    width = own_ref.shape[0] // 3
    nt = (((1,), (1,)), ((), ()))
    main = width * CAP // PAD
    step = width - main
    extra = PAD - CAP
    pieces = []
    for c in range(0, width, step):
        total = jnp.zeros((left_ref.shape[0], step), F32)
        for i in range(4):
            pack = (own_ref, near_ref)[i // 2]
            right = pack[i % 2 * width + c : i % 2 * width + c + step]
            left = left_ref[:, i * hidden : (i + 1) * hidden]
            total = total + lax.dot_general(left, right, nt, preferred_element_type=F32)
        pieces.append(total)
    last = pieces[-1]
    each = outs[0].shape[0] // PAD
    for i in range(left_ref.shape[0] // CAP):
        base = i * CAP
        out_ref, at = outs[i // each], i % each * PAD
        for j, piece in enumerate(pieces[:-1]):
            under = last[base + extra * j : base + extra * (j + 1)]
            both = jnp.concatenate([piece[base : base + CAP], under], axis=0)
            out_ref[at : at + PAD, j * step : (j + 1) * step] = both.astype(out_ref.dtype)


def attach_kernel(part_ref, *refs):
    outs = refs[len(refs) // 2 :]
    part = part_ref[...].astype(F32)
    lane = lax.broadcasted_iota(jnp.int32, part.shape, 1)
    each = outs[0].shape[0] // PAD
    for i in range(len(outs) * each):
        out_ref, at = outs[i // each], i % each * PAD
        tail = jnp.where(lane // 2 == i, part, 0.0)
        out_ref[at : at + PAD, out_ref.shape[1] - LANES :] = tail.astype(out_ref.dtype)


def add_kernel(keep_ref, got_ref, out_ref):
    main = keep_ref.shape[1] - LANES
    lane = lax.broadcasted_iota(jnp.int32, (PAD, LANES), 1)
    for i in range(2):
        rows = pl.ds(i * PAD, PAD)
        total = keep_ref[rows] + got_ref[rows].astype(F32)
        out_ref[rows, :main] = total[:, :main].astype(BF)
        high, low = split(jnp.sum(total[:, main:], axis=1, keepdims=True))
        tail = jnp.where(lane == 0, high.astype(F32), jnp.where(lane == 1, low.astype(F32), 0.0))
        out_ref[rows, main:] = tail.astype(BF)


def other_kernel(*refs):
    half = len(refs) - 1
    for k, ref in zip(reversed(range(half)), refs):
        refs[-1][k * PAD : (k + 1) * PAD] = ref[PAD:]


def mix_kernel(flight, ids_ref, place_ref, mix_ref, near_ref, *refs):
    half = flight // 2
    home, (out_ref, gates_ref) = refs[:half], refs[half:]
    home = home[::-1]
    blocks = []
    for k in range(half):
        blocks += [home[k].at[pl.ds(0, PAD)], near_ref.at[pl.ds(k * PAD, PAD)]]
    count, width = out_ref.shape
    main = width * CAP // PAD
    step = width - main
    tn = (((0,), (0,)), ((), ()))
    left = jnp.concatenate(
        [
            mix_ref[:, (2 * s + i) * count : (2 * s + i + 1) * count]
            for i in range(2)
            for s in range(flight)
        ],
        axis=0,
    )

    def blend(rows):
        right = jnp.concatenate([rows, rows], axis=0)
        return lax.dot_general(left, right, tn, preferred_element_type=F32).astype(BF)

    out_ref[:, :main] = blend(jnp.concatenate([b[:, :main] for b in blocks], axis=0))
    zero = jnp.zeros((PAD - CAP, step), BF)
    folded = []
    for s in range(flight):
        for j in range(main // step):
            folded.append(blocks[s][CAP:, j * step : (j + 1) * step])
        folded.append(zero)
    out_ref[:, main:] = blend(jnp.concatenate(folded, axis=0))
    own = lax.axis_index("expert") // SLICES
    parity = lax.axis_index("expert") % 2
    ids = ids_ref[...]
    total = jnp.zeros(ids.shape, F32)
    for s in range(flight):
        q = jnp.sum(blocks[s][:, main:].astype(F32), axis=1, keepdims=True)
        back = jnp.sum(place_ref[s * PAD : (s + 1) * PAD] * q, axis=0, keepdims=True)
        total = total + jnp.where(ids == (own ^ s ^ parity), back, 0.0)
    gates_ref[...] = total


def moved(value, sections, devices, stage, flip, bits, along=0):
    route = []
    for p in range(sections):
        for e in range(devices):
            there = e ^ bits ^ (along + SLICES * ((e ^ bits) % 2) if along is not None else 0)
            route.append((p * devices + e, (p + flip) % sections * devices + there))
    return lax.ppermute(value, stage, route)


def per_device(inputs, out_grads, expert_ids, gate_values, w_gate, w_up, w_down):
    devices = lax.axis_size("expert")
    sections = lax.axis_size("pipe")
    flight = devices // SLICES
    half = flight // 2
    count, width = inputs.shape[1:]
    go = functools.partial(moved, sections=sections, devices=devices, stage=("pipe", "expert"))
    ids = expert_ids[0].T
    gates = gate_values[0].T
    hidden = w_gate.shape[2]
    shape = jax.ShapeDtypeStruct
    main = width * CAP // PAD
    hbm = [pl.BlockSpec(memory_space=pltpu.HBM)]
    args = (ids, gates, inputs[0], out_grads[0], w_gate[0], w_up[0], w_down[0])
    *blocks, mix, place, pack = pl.pallas_call(
        functools.partial(select_kernel, flight),
        out_shape=[shape((2 * CAP, width), BF)] * flight
        + [
            shape((PAD, 2 * flight * count), BF),
            shape((flight * PAD, count), F32),
            shape((3 * width, hidden), BF),
        ],
        in_specs=hbm * 7,
        scratch_shapes=[
            pltpu.VMEM(ids.shape, jnp.int32),
            pltpu.VMEM(gates.shape, F32),
            pltpu.VMEM((count, width), BF),
            pltpu.VMEM((count, width), BF),
            pltpu.SemaphoreType.DMA((4,)),
            pltpu.SemaphoreType.DMA((2 + width // hidden,)),
        ],
        compiler_params=PARAMS,
        name="select",
    )(*[pltpu.with_memory_space_constraint(v, pltpu.HBM) for v in args])
    mine, theirs = blocks[:half], blocks[half:]
    rows = []
    for k in range(half):
        rows.append(go(mine[k], flip=0, bits=0, along=2 * k * SLICES))
        rows.append(go(theirs[k], flip=0, bits=1, along=2 * k * SLICES))
    near = go(pack, flip=0, bits=1, along=None)
    rows[-1], near = lax.optimization_barrier((rows[-1], near))
    rows = rows + [go(r, flip=0, bits=2, along=None) for r in rows]
    order = [*ORDER[0], *range(4, flight), *(flight + i for i in ORDER[1]), *range(flight + 4, 2 * flight)]
    left, part = pl.pallas_call(
        functools.partial(hidden_kernel, order),
        out_shape=[shape((2 * flight * CAP, 4 * hidden), BF), shape((PAD, LANES), BF)],
        compiler_params=PARAMS,
        name="hidden",
    )(*[rows[i] for i in order], pack, near)
    part = go(part, flip=1, bits=0, along=None)
    r_shapes = [shape((2 * PAD, main + LANES), t) for t in [F32] * half + [BF] * half]
    r_sums = pl.pallas_call(
        inputs_kernel,
        out_shape=r_shapes,
        compiler_params=PARAMS,
        name="inputs_back",
    )(left, pack, near)
    r_sums = pl.pallas_call(
        attach_kernel,
        out_shape=r_shapes,
        input_output_aliases={i + 1: i for i in range(2 * half)},
        compiler_params=PARAMS,
        name="attach_gate_parts",
    )(part, *r_sums)
    r_home = []
    for k in range(half):
        r_got = go(r_sums[half + k], flip=0, bits=2, along=None)
        r_part = pl.pallas_call(
            add_kernel,
            out_shape=shape((2 * PAD, main + LANES), BF),
            compiler_params=PARAMS,
            name="add_inputs_back",
        )(r_sums[k], r_got)
        r_home.append(go(r_part, flip=-1, bits=0, along=2 * k * SLICES))
    far_mix = go(mix, flip=-1, bits=0, along=None)
    r_home[-1], far_mix = lax.optimization_barrier((r_home[-1], far_mix))
    others = pl.pallas_call(
        other_kernel,
        out_shape=shape((half * PAD, main + LANES), BF),
        compiler_params=PARAMS,
        name="other_core",
    )(*r_home[::-1])
    r_near = go(others, flip=0, bits=1, along=None)
    moe, d_gates = pl.pallas_call(
        functools.partial(mix_kernel, flight),
        out_shape=[shape((count, width), BF), shape(ids.shape, F32)],
        compiler_params=PARAMS,
        name="mix",
    )(ids, place, far_mix, r_near, *r_home[::-1])
    return (moe[None], d_gates.T[None])


def solution(mesh):
    return jax.shard_map(
        per_device,
        mesh=mesh,
        in_specs=(
            P("pipe", "expert", None),
            P("pipe", "expert", None),
            P("pipe", "expert", None),
            P("pipe", "expert", None),
            P("pipe", None, "expert"),
            P("pipe", None, "expert"),
            P("pipe", "expert", None),
        ),
        out_specs=(P("pipe", "expert", None), P("pipe", "expert", None)),
        check_vma=False,
    )
```

```python
import functools

import jax
import jax.numpy as jnp
from jax import lax
from jax.experimental import pallas as pl
from jax.experimental.pallas import tpu as pltpu
from jax.sharding import PartitionSpec as P

SLICES = 4
CAP = 12
PAD = 16
LANES = 128
ORDER = ((1, 3, 2, 0), (1, 0, 3, 2))
BF = jnp.bfloat16
F32 = jnp.float32
PARAMS = pltpu.CompilerParams(vmem_limit_bytes=40 * 1024 * 1024)


def split(value):
    high = value.astype(BF)
    return high, (value - high.astype(F32)).astype(BF)


def weight_copies(wg_hbm, wu_hbm, wd_hbm, pack_ref, sems):
    width, hidden = wg_hbm.shape
    copies = [
        pltpu.make_async_copy(wg_hbm, pack_ref.at[pl.ds(0, width)], sems.at[0]),
        pltpu.make_async_copy(wu_hbm, pack_ref.at[pl.ds(width, width)], sems.at[1]),
    ]
    for k in range(width // hidden):
        part = pack_ref.at[pl.ds(2 * width + k * hidden, hidden)]
        copies.append(pltpu.make_async_copy(wd_hbm.at[:, pl.ds(k * hidden, hidden)], part, sems.at[2 + k]))
    return copies


def select_kernel(flight, ids_hbm, gates_hbm, x_hbm, g_hbm, wg_hbm, wu_hbm, wd_hbm, *refs):
    blocks, (mix_ref, place_ref, pack_ref) = refs[:flight], refs[flight : flight + 3]
    ids_ref, gates_ref, x_ref, g_ref, sems, pack_sems = refs[flight + 3 :]
    later = weight_copies(wg_hbm, wu_hbm, wd_hbm, pack_ref, pack_sems)
    first = [
        pltpu.make_async_copy(src, dst, sems.at[i])
        for i, (src, dst) in enumerate(
            [(ids_hbm, ids_ref), (gates_hbm, gates_ref), (x_hbm, x_ref), (g_hbm, g_ref)]
        )
    ]
    for copy in first:
        copy.start()
    for copy in later:
        copy.start(priority=1)
    own = lax.axis_index("expert") // SLICES
    parity = lax.axis_index("expert") % 2
    first[0].wait()
    first[1].wait()
    ids = ids_ref[...]
    gates = gates_ref[...]
    count = ids.shape[1]
    routed, weight = [], []
    for s in range(flight):
        match = ids == (own ^ s ^ parity)
        routed.append(jnp.sum(jnp.where(match, 1.0, 0.0), axis=0, keepdims=True))
        weight.append(jnp.sum(jnp.where(match, gates, 0.0), axis=0, keepdims=True))
    fill = [jnp.zeros((1, count), F32)] * (-flight % 8)
    table = jnp.concatenate(routed + fill, axis=0)
    earlier = lax.broadcasted_iota(jnp.int32, (count, count), 0) < lax.broadcasted_iota(
        jnp.int32, (count, count), 1
    )
    rank = jnp.dot(
        table.astype(BF), jnp.where(earlier, 1.0, 0.0).astype(BF), preferred_element_type=F32
    )
    key = jnp.where((table > 0.0) & (rank < float(CAP)), rank, -1.0)
    row = lax.broadcasted_iota(jnp.int32, (2 * CAP, count), 0)
    is_x = row < CAP
    slot = jnp.where(is_x, row, row - CAP).astype(F32)
    slot16 = lax.broadcasted_iota(jnp.int32, (PAD, count), 0)
    slot16 = jnp.where(slot16 < CAP, slot16, -2).astype(F32)
    picks_x, picks_g = [], []
    for s in [*range(0, flight, 2), *range(1, flight, 2)]:
        hit = key[s : s + 1] == slot
        picks_x.append(jnp.where(hit & is_x, 1.0, 0.0))
        picks_g.append(jnp.where(hit & ~is_x, 1.0, 0.0))
        at = jnp.where(key[s : s + 1] == slot16, 1.0, 0.0)
        place_ref[s * PAD : (s + 1) * PAD] = at
        for i, value in enumerate(split(at * weight[s])):
            mix_ref[:, (2 * s + i) * count : (2 * s + i + 1) * count] = value
    pick_x = jnp.concatenate(picks_x, axis=0).astype(BF)
    pick_g = jnp.concatenate(picks_g, axis=0).astype(BF)
    first[2].wait()
    rows = jnp.dot(pick_x, x_ref[...], preferred_element_type=F32)
    first[3].wait()
    rows = rows + jnp.dot(pick_g, g_ref[...], preferred_element_type=F32)
    rows = rows.astype(BF)
    for i in range(flight):
        blocks[i][...] = rows[i * 2 * CAP : (i + 1) * 2 * CAP]
    for copy in later:
        copy.wait()


def hidden_kernel(order, *refs):
    many = len(order)
    blocks, packs = refs[:many], refs[many : many + 2]
    left_ref, part_ref = refs[many + 2 :]
    blocks = [blocks[order.index(i)] for i in range(many)]
    step = 2 * CAP
    spots = [(b, at) for b in blocks for at in range(0, b.shape[0], step)]
    x = jnp.concatenate([b[at : at + CAP] for b, at in spots], axis=0)
    g = jnp.concatenate([b[at + CAP : at + step] for b, at in spots], axis=0)
    width = x.shape[1]
    hidden = packs[0].shape[1]
    nt = (((1,), (1,)), ((), ()))
    part = jnp.zeros((x.shape[0], 1), F32)
    for half, pack in enumerate(packs):
        a = jnp.dot(x, pack[:width], preferred_element_type=F32)
        u = jnp.dot(x, pack[width : 2 * width], preferred_element_type=F32)
        dh = jnp.zeros_like(a)
        for k in range(0, width, hidden):
            down = pack[2 * width + k : 2 * width + k + hidden]
            dh = dh + lax.dot_general(g[:, k : k + hidden], down, nt, preferred_element_type=F32)
        sig = jax.nn.sigmoid(a)
        act = a * sig
        part = part + jnp.sum(act * u * dh, axis=1, keepdims=True)
        at = 2 * half * hidden
        left_ref[:, at : at + hidden] = (dh * u * sig * (1.0 + a * (1.0 - sig))).astype(BF)
        left_ref[:, at + hidden : at + 2 * hidden] = (dh * act).astype(BF)
    high, low = split(part)
    high, low = high.astype(F32), low.astype(F32)
    lane = lax.broadcasted_iota(jnp.int32, (CAP, LANES), 1)
    tail = jnp.zeros((CAP, LANES), F32)
    for i in range(len(spots)):
        rows = slice(i * CAP, (i + 1) * CAP)
        tail = jnp.where(lane == 2 * i, high[rows], jnp.where(lane == 2 * i + 1, low[rows], tail))
    part_ref[...] = jnp.concatenate([tail, jnp.zeros((PAD - CAP, LANES), F32)], axis=0).astype(BF)


def inputs_kernel(left_ref, own_ref, near_ref, *outs):
    hidden = own_ref.shape[1]
    width = own_ref.shape[0] // 3
    nt = (((1,), (1,)), ((), ()))
    main = width * CAP // PAD
    step = width - main
    extra = PAD - CAP
    pieces = []
    for c in range(0, width, step):
        total = jnp.zeros((left_ref.shape[0], step), F32)
        for i in range(4):
            pack = (own_ref, near_ref)[i // 2]
            right = pack[i % 2 * width + c : i % 2 * width + c + step]
            left = left_ref[:, i * hidden : (i + 1) * hidden]
            total = total + lax.dot_general(left, right, nt, preferred_element_type=F32)
        pieces.append(total)
    last = pieces[-1]
    for i in range(left_ref.shape[0] // CAP):
        base = i * CAP
        out_ref, at = outs[i // 2], i % 2 * main
        for j, piece in enumerate(pieces[:-1]):
            under = last[base + extra * j : base + extra * (j + 1)]
            both = jnp.concatenate([piece[base : base + CAP], under], axis=0)
            out_ref[:, at + j * step : at + (j + 1) * step] = both.astype(out_ref.dtype)


def attach_kernel(part_ref, *refs):
    part = part_ref[...].astype(F32)
    lane = lax.broadcasted_iota(jnp.int32, part.shape, 1)
    for i, out_ref in enumerate(refs[len(refs) // 2 :]):
        tail = jnp.where(lane // 4 == i, part, 0.0)
        out_ref[:, out_ref.shape[1] - LANES :] = tail.astype(out_ref.dtype)


def add_kernel(keep_ref, got_ref, out_ref):
    both = keep_ref.shape[1] - LANES
    lane = lax.broadcasted_iota(jnp.int32, (PAD, LANES), 1)
    total = keep_ref[...] + got_ref[...].astype(F32)
    out_ref[:, :both] = total[:, :both].astype(BF)
    tail = jnp.zeros((PAD, LANES), F32)
    for o in range(2):
        mine = jnp.where(lane // 2 % 2 == o, total[:, both:], 0.0)
        high, low = split(jnp.sum(mine, axis=1, keepdims=True))
        tail = jnp.where(lane == 2 * o, high.astype(F32), tail)
        tail = jnp.where(lane == 2 * o + 1, low.astype(F32), tail)
    out_ref[:, both:] = tail.astype(BF)


def other_kernel(*refs):
    half = len(refs) - 1
    main = refs[-1].shape[1] - LANES
    for k, ref in zip(reversed(range(half)), refs):
        refs[-1][k * PAD : (k + 1) * PAD] = ref[:, main:]


def mix_kernel(flight, ids_ref, place_ref, mix_ref, near_ref, *refs):
    half = flight // 2
    home, (out_ref, gates_ref) = refs[:half], refs[half:]
    home = home[::-1]
    blocks, tails = [], []
    count, width = out_ref.shape
    main = width * CAP // PAD
    step = width - main
    lane = lax.broadcasted_iota(jnp.int32, (PAD, LANES), 1)
    for k in range(half):
        near = near_ref.at[pl.ds(k * PAD, PAD)]
        blocks += [home[k], near]
        tails += [jnp.where(lane // 2 == o, v[...].astype(F32), 0.0) for o, v in enumerate((home[k].at[:, pl.ds(2 * main, LANES)], near.at[:, pl.ds(main, LANES)]))]
    tn = (((0,), (0,)), ((), ()))
    left = jnp.concatenate(
        [
            mix_ref[:, (2 * s + i) * count : (2 * s + i + 1) * count]
            for i in range(2)
            for s in range(flight)
        ],
        axis=0,
    )

    def blend(rows):
        right = jnp.concatenate([rows, rows], axis=0)
        return lax.dot_general(left, right, tn, preferred_element_type=F32).astype(BF)

    out_ref[:, :main] = blend(jnp.concatenate([b[:, :main] for b in blocks], axis=0))
    zero = jnp.zeros((PAD - CAP, step), BF)
    folded = []
    for s in range(flight):
        for j in range(main // step):
            folded.append(blocks[s][CAP:, j * step : (j + 1) * step])
        folded.append(zero)
    out_ref[:, main:] = blend(jnp.concatenate(folded, axis=0))
    own = lax.axis_index("expert") // SLICES
    parity = lax.axis_index("expert") % 2
    ids = ids_ref[...]
    total = jnp.zeros(ids.shape, F32)
    for s in range(flight):
        q = jnp.sum(tails[s], axis=1, keepdims=True)
        back = jnp.sum(place_ref[s * PAD : (s + 1) * PAD] * q, axis=0, keepdims=True)
        total = total + jnp.where(ids == (own ^ s ^ parity), back, 0.0)
    gates_ref[...] = total


def moved(value, sections, devices, stage, flip, bits, along=0):
    route = []
    for p in range(sections):
        for e in range(devices):
            there = e ^ bits ^ (along + SLICES * ((e ^ bits) % 2) if along is not None else 0)
            route.append((p * devices + e, (p + flip) % sections * devices + there))
    return lax.ppermute(value, stage, route)


def per_device(inputs, out_grads, expert_ids, gate_values, w_gate, w_up, w_down):
    devices = lax.axis_size("expert")
    sections = lax.axis_size("pipe")
    flight = devices // SLICES
    half = flight // 2
    count, width = inputs.shape[1:]
    go = functools.partial(moved, sections=sections, devices=devices, stage=("pipe", "expert"))
    ids = expert_ids[0].T
    gates = gate_values[0].T
    hidden = w_gate.shape[2]
    shape = jax.ShapeDtypeStruct
    main = width * CAP // PAD
    hbm = [pl.BlockSpec(memory_space=pltpu.HBM)]
    args = (ids, gates, inputs[0], out_grads[0], w_gate[0], w_up[0], w_down[0])
    *blocks, mix, place, pack = pl.pallas_call(
        functools.partial(select_kernel, flight),
        out_shape=[shape((2 * CAP, width), BF)] * flight
        + [
            shape((PAD, 2 * flight * count), BF),
            shape((flight * PAD, count), F32),
            shape((3 * width, hidden), BF),
        ],
        in_specs=hbm * 7,
        scratch_shapes=[
            pltpu.VMEM(ids.shape, jnp.int32),
            pltpu.VMEM(gates.shape, F32),
            pltpu.VMEM((count, width), BF),
            pltpu.VMEM((count, width), BF),
            pltpu.SemaphoreType.DMA((4,)),
            pltpu.SemaphoreType.DMA((2 + width // hidden,)),
        ],
        compiler_params=PARAMS,
        name="select",
    )(*[pltpu.with_memory_space_constraint(v, pltpu.HBM) for v in args])
    mine, theirs = blocks[:half], blocks[half:]
    rows = []
    for k in range(half):
        rows.append(go(mine[k], flip=0, bits=0, along=2 * k * SLICES))
        rows.append(go(theirs[k], flip=0, bits=1, along=2 * k * SLICES))
    near = go(pack, flip=0, bits=1, along=None)
    rows[-1], near = lax.optimization_barrier((rows[-1], near))
    rows = rows + [go(r, flip=0, bits=2, along=None) for r in rows]
    order = [*ORDER[0], *range(4, flight), *(flight + i for i in ORDER[1]), *range(flight + 4, 2 * flight)]
    left, part = pl.pallas_call(
        functools.partial(hidden_kernel, order),
        out_shape=[shape((2 * flight * CAP, 4 * hidden), BF), shape((PAD, LANES), BF)],
        compiler_params=PARAMS,
        name="hidden",
    )(*[rows[i] for i in order], pack, near)
    part = go(part, flip=1, bits=0, along=None)
    r_shapes = [shape((PAD, 2 * main + LANES), t) for t in [F32] * half + [BF] * half]
    r_sums = pl.pallas_call(
        inputs_kernel,
        out_shape=r_shapes,
        compiler_params=PARAMS,
        name="inputs_back",
    )(left, pack, near)
    r_sums = pl.pallas_call(
        attach_kernel,
        out_shape=r_shapes,
        input_output_aliases={i + 1: i for i in range(2 * half)},
        compiler_params=PARAMS,
        name="attach_gate_parts",
    )(part, *r_sums)
    r_home = []
    for k in range(half):
        r_got = go(r_sums[half + k], flip=0, bits=2, along=None)
        r_part = pl.pallas_call(
            add_kernel,
            out_shape=shape((PAD, 2 * main + LANES), BF),
            compiler_params=PARAMS,
            name="add_inputs_back",
        )(r_sums[k], r_got)
        r_home.append(go(r_part, flip=-1, bits=0, along=2 * k * SLICES))
    far_mix = go(mix, flip=-1, bits=0, along=None)
    r_home[-1], far_mix = lax.optimization_barrier((r_home[-1], far_mix))
    others = pl.pallas_call(
        other_kernel,
        out_shape=shape((half * PAD, main + LANES), BF),
        compiler_params=PARAMS,
        name="other_core",
    )(*r_home[::-1])
    r_near = go(others, flip=0, bits=1, along=None)
    moe, d_gates = pl.pallas_call(
        functools.partial(mix_kernel, flight),
        out_shape=[shape((count, width), BF), shape(ids.shape, F32)],
        compiler_params=PARAMS,
        name="mix",
    )(ids, place, far_mix, r_near, *r_home[::-1])
    return (moe[None], d_gates.T[None])


def solution(mesh):
    return jax.shard_map(
        per_device,
        mesh=mesh,
        in_specs=(
            P("pipe", "expert", None),
            P("pipe", "expert", None),
            P("pipe", "expert", None),
            P("pipe", "expert", None),
            P("pipe", None, "expert"),
            P("pipe", None, "expert"),
            P("pipe", "expert", None),
        ),
        out_specs=(P("pipe", "expert", None), P("pipe", "expert", None)),
        check_vma=False,
    )
```

```python
import functools

import jax
import jax.numpy as jnp
from jax import lax
from jax.experimental import pallas as pl
from jax.experimental.pallas import tpu as pltpu
from jax.sharding import PartitionSpec as P

SLICES = 4
CAP = 12
PAD = 16
LANES = 128
ORDER = ((1, 3, 2, 0), (1, 0, 3, 2))
BF = jnp.bfloat16
F32 = jnp.float32
PARAMS = pltpu.CompilerParams(vmem_limit_bytes=40 * 1024 * 1024)


def split(value):
    high = value.astype(BF)
    return high, (value - high.astype(F32)).astype(BF)


def weight_copies(wg_hbm, wu_hbm, wd_hbm, pack_ref, sems):
    width, hidden = wg_hbm.shape
    copies = [
        pltpu.make_async_copy(wg_hbm, pack_ref.at[pl.ds(0, width)], sems.at[0]),
        pltpu.make_async_copy(wu_hbm, pack_ref.at[pl.ds(width, width)], sems.at[1]),
    ]
    for k in range(width // hidden):
        part = pack_ref.at[pl.ds(2 * width + k * hidden, hidden)]
        copies.append(pltpu.make_async_copy(wd_hbm.at[:, pl.ds(k * hidden, hidden)], part, sems.at[2 + k]))
    return copies


def select_kernel(flight, ids_hbm, gates_hbm, x_hbm, g_hbm, wg_hbm, wu_hbm, wd_hbm, *refs):
    blocks, (mix_ref, place_ref, pack_ref) = refs[:flight], refs[flight : flight + 3]
    ids_ref, gates_ref, x_ref, g_ref, sems, pack_sems = refs[flight + 3 :]
    later = weight_copies(wg_hbm, wu_hbm, wd_hbm, pack_ref, pack_sems)
    first = [
        pltpu.make_async_copy(src, dst, sems.at[i])
        for i, (src, dst) in enumerate(
            [(ids_hbm, ids_ref), (gates_hbm, gates_ref), (x_hbm, x_ref), (g_hbm, g_ref)]
        )
    ]
    for copy in first:
        copy.start()
    for copy in later:
        copy.start(priority=1)
    own = lax.axis_index("expert") // SLICES
    parity = lax.axis_index("expert") % 2
    first[0].wait()
    first[1].wait()
    ids = ids_ref[...]
    gates = gates_ref[...]
    count = ids.shape[1]
    routed, weight = [], []
    for s in range(flight):
        match = ids == (own ^ s ^ parity)
        routed.append(jnp.sum(jnp.where(match, 1.0, 0.0), axis=0, keepdims=True))
        weight.append(jnp.sum(jnp.where(match, gates, 0.0), axis=0, keepdims=True))
    fill = [jnp.zeros((1, count), F32)] * (-flight % 8)
    table = jnp.concatenate(routed + fill, axis=0)
    earlier = lax.broadcasted_iota(jnp.int32, (count, count), 0) < lax.broadcasted_iota(
        jnp.int32, (count, count), 1
    )
    rank = jnp.dot(
        table.astype(BF), jnp.where(earlier, 1.0, 0.0).astype(BF), preferred_element_type=F32
    )
    key = jnp.where((table > 0.0) & (rank < float(CAP)), rank, -1.0)
    row = lax.broadcasted_iota(jnp.int32, (2 * CAP, count), 0)
    is_x = row < CAP
    slot = jnp.where(is_x, row, row - CAP).astype(F32)
    slot16 = lax.broadcasted_iota(jnp.int32, (PAD, count), 0)
    slot16 = jnp.where(slot16 < CAP, slot16, -2).astype(F32)
    picks_x, picks_g = [], []
    for s in [*range(0, flight, 2), *range(1, flight, 2)]:
        hit = key[s : s + 1] == slot
        picks_x.append(jnp.where(hit & is_x, 1.0, 0.0))
        picks_g.append(jnp.where(hit & ~is_x, 1.0, 0.0))
        at = jnp.where(key[s : s + 1] == slot16, 1.0, 0.0)
        place_ref[s * PAD : (s + 1) * PAD] = at
        for i, value in enumerate(split(at * weight[s])):
            mix_ref[:, (2 * s + i) * count : (2 * s + i + 1) * count] = value
    pick_x = jnp.concatenate(picks_x, axis=0).astype(BF)
    pick_g = jnp.concatenate(picks_g, axis=0).astype(BF)
    first[2].wait()
    rows = jnp.dot(pick_x, x_ref[...], preferred_element_type=F32)
    first[3].wait()
    rows = rows + jnp.dot(pick_g, g_ref[...], preferred_element_type=F32)
    rows = rows.astype(BF)
    for i in range(flight):
        blocks[i][...] = rows[i * 2 * CAP : (i + 1) * 2 * CAP]
    for copy in later:
        copy.wait()


def hidden_kernel(order, *refs):
    many = len(order)
    blocks, packs = refs[:many], refs[many : many + 2]
    left_ref, part_ref = refs[many + 2 :]
    blocks = [blocks[order.index(i)] for i in range(many)]
    step = 2 * CAP
    spots = [(b, at) for b in blocks for at in range(0, b.shape[0], step)]
    x = jnp.concatenate([b[at : at + CAP] for b, at in spots], axis=0)
    g = jnp.concatenate([b[at + CAP : at + step] for b, at in spots], axis=0)
    width = x.shape[1]
    hidden = packs[0].shape[1]
    nt = (((1,), (1,)), ((), ()))
    part = jnp.zeros((x.shape[0], 1), F32)
    for half, pack in enumerate(packs):
        a = jnp.dot(x, pack[:width], preferred_element_type=F32)
        u = jnp.dot(x, pack[width : 2 * width], preferred_element_type=F32)
        dh = jnp.zeros_like(a)
        for k in range(0, width, hidden):
            down = pack[2 * width + k : 2 * width + k + hidden]
            dh = dh + lax.dot_general(g[:, k : k + hidden], down, nt, preferred_element_type=F32)
        sig = jax.nn.sigmoid(a)
        act = a * sig
        part = part + jnp.sum(act * u * dh, axis=1, keepdims=True)
        at = 2 * half * hidden
        left_ref[:, at : at + hidden] = (dh * u * sig * (1.0 + a * (1.0 - sig))).astype(BF)
        left_ref[:, at + hidden : at + 2 * hidden] = (dh * act).astype(BF)
    high, low = split(part)
    high, low = high.astype(F32), low.astype(F32)
    lane = lax.broadcasted_iota(jnp.int32, (CAP, LANES), 1)
    tail = jnp.zeros((CAP, LANES), F32)
    for i in range(len(spots)):
        rows = slice(i * CAP, (i + 1) * CAP)
        tail = jnp.where(lane == 2 * i, high[rows], jnp.where(lane == 2 * i + 1, low[rows], tail))
    part_ref[...] = jnp.concatenate([tail, jnp.zeros((PAD - CAP, LANES), F32)], axis=0).astype(BF)


def inputs_kernel(left_ref, own_ref, near_ref, *outs):
    hidden = own_ref.shape[1]
    width = own_ref.shape[0] // 3
    nt = (((1,), (1,)), ((), ()))
    main = width * CAP // PAD
    step = width - main
    extra = PAD - CAP
    pieces = []
    for c in range(0, width, step):
        total = jnp.zeros((left_ref.shape[0], step), F32)
        for i in range(4):
            pack = (own_ref, near_ref)[i // 2]
            right = pack[i % 2 * width + c : i % 2 * width + c + step]
            left = left_ref[:, i * hidden : (i + 1) * hidden]
            total = total + lax.dot_general(left, right, nt, preferred_element_type=F32)
        pieces.append(total)
    last = pieces[-1]
    for i in range(left_ref.shape[0] // CAP):
        base = i * CAP
        out_ref, at = outs[i // 2], i % 2 * main
        for j, piece in enumerate(pieces[:-1]):
            under = last[base + extra * j : base + extra * (j + 1)]
            both = jnp.concatenate([piece[base : base + CAP], under], axis=0)
            out_ref[:, at + j * step : at + (j + 1) * step] = both.astype(out_ref.dtype)


def attach_kernel(part_ref, *refs):
    part = part_ref[...].astype(F32)
    lane = lax.broadcasted_iota(jnp.int32, part.shape, 1)
    for i, out_ref in enumerate(refs[len(refs) // 2 :]):
        tail = jnp.where(lane // 4 == i, part, 0.0)
        out_ref[:, out_ref.shape[1] - LANES :] = tail.astype(out_ref.dtype)


def add_kernel(keep_ref, got_ref, out_ref):
    both = keep_ref.shape[1] - LANES
    lane = lax.broadcasted_iota(jnp.int32, (PAD, LANES), 1)
    total = keep_ref[...] + got_ref[...].astype(F32)
    out_ref[:, :both] = total[:, :both].astype(BF)
    tail = jnp.zeros((PAD, LANES), F32)
    for o in range(2):
        mine = jnp.where(lane // 2 % 2 == o, total[:, both:], 0.0)
        high, low = split(jnp.sum(mine, axis=1, keepdims=True))
        tail = jnp.where(lane == 2 * o, high.astype(F32), tail)
        tail = jnp.where(lane == 2 * o + 1, low.astype(F32), tail)
    out_ref[:, both:] = tail.astype(BF)


def other_kernel(*refs):
    half = len(refs) - 1
    main = refs[-1].shape[1] - LANES
    for k, ref in zip(reversed(range(half)), refs):
        refs[-1][k * PAD : (k + 1) * PAD] = ref[:, main:]


def mix_kernel(flight, ids_ref, place_ref, mix_ref, near_ref, *refs):
    half = flight // 2
    home, (out_hbm, gates_ref, out_ref, sems) = refs[:half], refs[half:]
    home = home[::-1]
    blocks, tails = [], []
    count, width = out_ref.shape
    main = width * CAP // PAD
    step = width - main
    lane = lax.broadcasted_iota(jnp.int32, (PAD, LANES), 1)
    for k in range(half):
        near = near_ref.at[pl.ds(k * PAD, PAD)]
        blocks += [home[k], near]
        tails += [jnp.where(lane // 2 == o, v[...].astype(F32), 0.0) for o, v in enumerate((home[k].at[:, pl.ds(2 * main, LANES)], near.at[:, pl.ds(main, LANES)]))]
    tn = (((0,), (0,)), ((), ()))
    left = jnp.concatenate(
        [
            mix_ref[:, (2 * s + i) * count : (2 * s + i + 1) * count]
            for i in range(2)
            for s in range(flight)
        ],
        axis=0,
    )

    def blend(rows):
        right = jnp.concatenate([rows, rows], axis=0)
        return lax.dot_general(left, right, tn, preferred_element_type=F32).astype(BF)

    copies = []

    def store(rows, at):
        cols = pl.ds(at, step)
        out_ref[:, cols] = blend(rows)
        copies.append(pltpu.make_async_copy(out_ref.at[:, cols], out_hbm.at[:, cols], sems.at[at // step]))
        copies[-1].start()

    for c in range(0, main, step):
        store(jnp.concatenate([b[:, c : c + step] for b in blocks], axis=0), c)
    zero = jnp.zeros((PAD - CAP, step), BF)
    folded = []
    for s in range(flight):
        for j in range(main // step):
            folded.append(blocks[s][CAP:, j * step : (j + 1) * step])
        folded.append(zero)
    store(jnp.concatenate(folded, axis=0), main)
    own = lax.axis_index("expert") // SLICES
    parity = lax.axis_index("expert") % 2
    ids = ids_ref[...]
    total = jnp.zeros(ids.shape, F32)
    for s in range(flight):
        q = jnp.sum(tails[s], axis=1, keepdims=True)
        back = jnp.sum(place_ref[s * PAD : (s + 1) * PAD] * q, axis=0, keepdims=True)
        total = total + jnp.where(ids == (own ^ s ^ parity), back, 0.0)
    gates_ref[...] = total
    for copy in copies:
        copy.wait()


def moved(value, sections, devices, stage, flip, bits, along=0):
    route = []
    for p in range(sections):
        for e in range(devices):
            there = e ^ bits ^ (along + SLICES * ((e ^ bits) % 2) if along is not None else 0)
            route.append((p * devices + e, (p + flip) % sections * devices + there))
    return lax.ppermute(value, stage, route)


def per_device(inputs, out_grads, expert_ids, gate_values, w_gate, w_up, w_down):
    devices = lax.axis_size("expert")
    sections = lax.axis_size("pipe")
    flight = devices // SLICES
    half = flight // 2
    count, width = inputs.shape[1:]
    go = functools.partial(moved, sections=sections, devices=devices, stage=("pipe", "expert"))
    ids = expert_ids[0].T
    gates = gate_values[0].T
    hidden = w_gate.shape[2]
    shape = jax.ShapeDtypeStruct
    main = width * CAP // PAD
    hbm = [pl.BlockSpec(memory_space=pltpu.HBM)]
    args = (ids, gates, inputs[0], out_grads[0], w_gate[0], w_up[0], w_down[0])
    *blocks, mix, place, pack = pl.pallas_call(
        functools.partial(select_kernel, flight),
        out_shape=[shape((2 * CAP, width), BF)] * flight
        + [
            shape((PAD, 2 * flight * count), BF),
            shape((flight * PAD, count), F32),
            shape((3 * width, hidden), BF),
        ],
        in_specs=hbm * 7,
        scratch_shapes=[
            pltpu.VMEM(ids.shape, jnp.int32),
            pltpu.VMEM(gates.shape, F32),
            pltpu.VMEM((count, width), BF),
            pltpu.VMEM((count, width), BF),
            pltpu.SemaphoreType.DMA((4,)),
            pltpu.SemaphoreType.DMA((2 + width // hidden,)),
        ],
        compiler_params=PARAMS,
        name="select",
    )(*[pltpu.with_memory_space_constraint(v, pltpu.HBM) for v in args])
    mine, theirs = blocks[:half], blocks[half:]
    rows = []
    for k in range(half):
        rows.append(go(mine[k], flip=0, bits=0, along=2 * k * SLICES))
        rows.append(go(theirs[k], flip=0, bits=1, along=2 * k * SLICES))
    near = go(pack, flip=0, bits=1, along=None)
    rows[-1], near = lax.optimization_barrier((rows[-1], near))
    rows = rows + [go(r, flip=0, bits=2, along=None) for r in rows]
    order = [*ORDER[0], *range(4, flight), *(flight + i for i in ORDER[1]), *range(flight + 4, 2 * flight)]
    left, part = pl.pallas_call(
        functools.partial(hidden_kernel, order),
        out_shape=[shape((2 * flight * CAP, 4 * hidden), BF), shape((PAD, LANES), BF)],
        compiler_params=PARAMS,
        name="hidden",
    )(*[rows[i] for i in order], pack, near)
    part = go(part, flip=1, bits=0, along=None)
    r_shapes = [shape((PAD, 2 * main + LANES), t) for t in [F32] * half + [BF] * half]
    r_sums = pl.pallas_call(
        inputs_kernel,
        out_shape=r_shapes,
        compiler_params=PARAMS,
        name="inputs_back",
    )(left, pack, near)
    r_sums = pl.pallas_call(
        attach_kernel,
        out_shape=r_shapes,
        input_output_aliases={i + 1: i for i in range(2 * half)},
        compiler_params=PARAMS,
        name="attach_gate_parts",
    )(part, *r_sums)
    r_home = []
    for k in range(half):
        r_got = go(r_sums[half + k], flip=0, bits=2, along=None)
        r_part = pl.pallas_call(
            add_kernel,
            out_shape=shape((PAD, 2 * main + LANES), BF),
            compiler_params=PARAMS,
            name="add_inputs_back",
        )(r_sums[k], r_got)
        r_home.append(go(r_part, flip=-1, bits=0, along=2 * k * SLICES))
    far_mix = go(mix, flip=-1, bits=0, along=None)
    r_home[-1], far_mix = lax.optimization_barrier((r_home[-1], far_mix))
    others = pl.pallas_call(
        other_kernel,
        out_shape=shape((half * PAD, main + LANES), BF),
        compiler_params=PARAMS,
        name="other_core",
    )(*r_home[::-1])
    r_near = go(others, flip=0, bits=1, along=None)
    moe, d_gates = pl.pallas_call(
        functools.partial(mix_kernel, flight),
        out_shape=[shape((count, width), BF), shape(ids.shape, F32)],
        out_specs=[*hbm, pl.BlockSpec(memory_space=pltpu.VMEM)],
        scratch_shapes=[
            pltpu.VMEM((count, width), BF),
            pltpu.SemaphoreType.DMA((width // (width - main),)),
        ],
        compiler_params=PARAMS,
        name="mix",
    )(ids, place, far_mix, r_near, *r_home[::-1])
    return (moe[None], d_gates.T[None])


def solution(mesh):
    return jax.shard_map(
        per_device,
        mesh=mesh,
        in_specs=(
            P("pipe", "expert", None),
            P("pipe", "expert", None),
            P("pipe", "expert", None),
            P("pipe", "expert", None),
            P("pipe", None, "expert"),
            P("pipe", None, "expert"),
            P("pipe", "expert", None),
        ),
        out_specs=(P("pipe", "expert", None), P("pipe", "expert", None)),
        check_vma=False,
    )
```
